256 devices in a mesh: grp: 8 (over x, z_hi), seq: 32 (over z_lo, y, core).
Axes of the slice: x: 4, y: 4, z: 8 (z_hi: 2, z_lo: 4; z = z_hi * 4 + z_lo), core: 2. Of those that a mesh axis runs over, the one named last changes fastest.
Arguments:
- rows_alpha: bfloat16 [3, 8192, 8192], P(None, 'grp', 'seq'), may hold values from -40 to 40
- rows_beta: bfloat16 [3, 8192, 8192], P(None, 'grp', 'seq'), may hold values from -40 to 40
- filter_alpha: float32 [8192, 128], P(('grp', 'seq')), may hold values from -1 to 1
- filter_beta: float32 [8192, 128], P(('grp', 'seq')), may hold values from -1 to 1
Outputs:
- correlation: float32 [8192, 8192], P(('grp', 'seq'))
The draws below stay inside these ranges and needn't reach their ends.
All inputs are finite; a program needn't handle non-finite values.
Results may differ from the reference program's by a relative error of at most 0.0038.
Values may be sent and summed in bfloat16 or wider, within the bound.
A program may use at most 128 MiB of HBM per device.

```python
import jax
import jax.numpy as jnp
import numpy as np
from jax import lax

D = 8192
FILT = 128
TOK_DEV = 256
TOKENS = 8192
N_SEQ = 32


def common_rows(key):
    return jax.random.normal(jax.random.fold_in(key, 101), (3, D, TOKENS), jnp.float32)


def common_filter(key):
    noise = jax.random.normal(jax.random.fold_in(key, 202), (D, FILT), jnp.float32)
    decay_rates = jnp.exp(jax.random.uniform(jax.random.fold_in(key, 303), (D, 1), jnp.float32, jnp.log(1.0 / 2000.0), jnp.log(1.0 / 30.0)))
    positions = jnp.arange(FILT, dtype=jnp.float32)[None, :]
    return (noise, jnp.exp(-decay_rates * positions))


def draw_rows_alpha(key, part):
    common = common_rows(key)
    key = jax.random.fold_in(key, 1)
    private = jax.random.normal(key, (3, D, TOKENS), jnp.float32)
    mixture = 0.9 * common + 0.44 * private
    return jnp.clip(mixture, -40.0, 40.0).astype(jnp.bfloat16)


def draw_rows_beta(key, part):
    common = common_rows(key)
    key = jax.random.fold_in(key, 2)
    private = jax.random.normal(key, (3, D, TOKENS), jnp.float32)
    mixture = 0.9 * common + 0.44 * private
    return jnp.clip(mixture, -40.0, 40.0).astype(jnp.bfloat16)


def draw_filter_alpha(key, part):
    common, envelope = common_filter(key)
    key = jax.random.fold_in(key, 3)
    private = jax.random.normal(key, (D, FILT), jnp.float32)
    return jnp.clip(0.15 * (0.8 * common + 0.6 * private) * envelope, -1.0, 1.0)


def draw_filter_beta(key, part):
    common, envelope = common_filter(key)
    key = jax.random.fold_in(key, 4)
    private = jax.random.normal(key, (D, FILT), jnp.float32)
    return jnp.clip(0.15 * (0.8 * common + 0.6 * private) * envelope, -1.0, 1.0)


def setup_inputs(seed: int = 0) -> dict:
    key_of = jax.random.split(jax.random.key(seed), 5)
    return {
        "rows_alpha": draw_rows_alpha(jax.random.fold_in(key_of[4], 71), 0),
        "rows_beta": draw_rows_beta(jax.random.fold_in(key_of[4], 71), 0),
        "filter_alpha": draw_filter_alpha(jax.random.fold_in(key_of[4], 71), 0),
        "filter_beta": draw_filter_beta(jax.random.fold_in(key_of[4], 71), 0),
    }


def toeplitz_pair(filter_taps):
    width = filter_taps.shape[1]
    row_index = np.arange(width)[:, None]
    col_index = np.arange(width)[None, :]
    tap_index = jnp.asarray((row_index - col_index) % width, dtype=jnp.int32)
    circulant = filter_taps[:, tap_index]
    lower = jnp.asarray(row_index - col_index >= 0)
    near_part = jnp.where(lower[None], circulant, jnp.float32(0.0))
    far_part = jnp.where(lower[None], jnp.float32(0.0), circulant)
    return (near_part, far_part)

def mix_conv(rows, filter_taps):
    channels = rows.shape[1]
    length_all = rows.shape[2]
    width = filter_taps.shape[1]
    query_part = rows[0].astype(jnp.float32)
    product = rows[1].astype(jnp.float32) * rows[2].astype(jnp.float32)
    blocks = product.reshape(channels, length_all // width, width)
    previous = jnp.pad(blocks, ((0, 0), (1, 0), (0, 0)))[:, :-1]
    near_part, far_part = toeplitz_pair(filter_taps)
    convolved = jnp.einsum('cab,cjb->cja', near_part, blocks, precision=lax.Precision.HIGHEST)
    convolved = convolved + jnp.einsum('cab,cjb->cja', far_part, previous, precision=lax.Precision.HIGHEST)
    gated_out = query_part * convolved.reshape(channels, length_all)
    average = lax.optimization_barrier(jnp.mean(gated_out, axis=1, keepdims=True))
    centred = gated_out - average
    variance = lax.optimization_barrier(jnp.mean(centred * centred, axis=1, keepdims=True))
    return (centred * lax.rsqrt(variance + 1e-05)).astype(jnp.bfloat16)

def standardize_all(rows, filter_taps):
    block_width = min(D, 256)
    block_count = D // block_width
    grouped = rows.reshape(3, block_count, block_width, TOKENS).transpose(1, 0, 2, 3)
    taps_grouped = filter_taps.reshape(block_count, block_width, FILT)
    result = lax.map(lambda pair: mix_conv(pair[0], pair[1]), (grouped, taps_grouped))
    return result.reshape(D, TOKENS)

def reference(rows_alpha, rows_beta, filter_alpha, filter_beta):
    z_alpha = standardize_all(rows_alpha, filter_alpha)
    z_beta = standardize_all(rows_beta, filter_beta)

    def accumulate(running, shard_idx):
        first_tok = (shard_idx * TOK_DEV).astype(jnp.int32)
        left_part = lax.dynamic_slice_in_dim(z_alpha, first_tok, TOK_DEV, 1)
        right_part = lax.dynamic_slice_in_dim(z_beta, first_tok, TOK_DEV, 1)
        partial_value = lax.dot_general(left_part, right_part, (((1,), (1,)), ((), ())), preferred_element_type=jnp.float32)
        return (running + partial_value * (1.0 / TOKENS), None)
    running, unused = lax.scan(accumulate, jnp.zeros((D, D), jnp.float32), jnp.arange(N_SEQ, dtype=jnp.int32))
    return running
```

```python
import functools

import jax
import jax.numpy as jnp
import ml_dtypes
import numpy as np
from jax import lax
from jax.experimental import pallas as pl
from jax.experimental.pallas import tpu as pltpu
from jax.sharding import PartitionSpec as P

MESH = pl.DeviceIdType.MESH
BF = jnp.bfloat16
F32 = jnp.float32
TOKENS = 8192
CHAN = 1024
TOK = 256
TAPS = 128
CHUNK = 256


def split_const(matrix):
    high = matrix.astype(ml_dtypes.bfloat16)
    low = (matrix - high.astype(np.float64)).astype(ml_dtypes.bfloat16)
    return high, low


def dft_constants():
    n = np.arange(256)[:, None]
    k = np.arange(128)[None, :] + 0.5
    angle = 2.0 * np.pi * n * k / 256.0
    forward = np.concatenate([np.cos(angle), -np.sin(angle)], axis=1)
    back = angle[128:].T
    inverse = np.concatenate([np.cos(back), -np.sin(back)], axis=0) / 128.0
    return split_const(forward) + split_const(inverse)


def split(value):
    high = value.astype(BF)
    low = (value - high.astype(F32)).astype(BF)
    return high, low


def dot3(value, w_high, w_low):
    high, low = split(value)
    total = jnp.dot(low, w_high, preferred_element_type=F32)
    total = total + jnp.dot(high, w_low, preferred_element_type=F32)
    return total + jnp.dot(high, w_high, preferred_element_type=F32)


def place():
    g = lax.axis_index("grp")
    s = lax.axis_index("seq")
    return g, s, g // 2, g % 2, s // 8, (s // 2) % 4, s % 2


def eye_mask():
    r = lax.broadcasted_iota(jnp.int32, (128, 128), 0)
    c = lax.broadcasted_iota(jnp.int32, (128, 128), 1)
    return r == c


def to_row(column, eye):
    return jnp.sum(jnp.where(eye, jnp.broadcast_to(column, (128, 128)), 0.0), axis=0, keepdims=True)


def to_column(row, eye):
    return jnp.sum(jnp.where(eye, jnp.broadcast_to(row, (128, 128)), 0.0), axis=1, keepdims=True)


def front_kernel(
    rows_a, rows_b, filt_a, filt_b, wf_hi, wf_lo, wi_hi, wi_lo, z_a, z_b,
    halo, taps, centred, own, level1, level2,
    h_send, h_recv, f1_send, f1_recv, f2_send, f2_recv, f3_send, f3_recv, s1_send, s1_recv, s2_send, s2_recv,
):
    g, s, _, _, zl, y, c = place()
    following = lax.rem(s + 1, 32)
    barrier = pltpu.get_barrier_semaphore()
    zl_peers = [lax.rem(zl + i, 4) for i in range(1, 4)]
    y_peers = [lax.rem(y + i, 4) for i in range(1, 4)]
    seq = lambda a, b, d: (g, a * 8 + b * 2 + d)
    pl.semaphore_signal(barrier, inc=1, device_id=(g, lax.rem(s + 31, 32)), device_id_type=MESH)
    for p in zl_peers:
        pl.semaphore_signal(barrier, inc=1, device_id=seq(p, y, c), device_id_type=MESH)
    for i in range(1, 8):
        q = lax.rem(y * 2 + c + i, 8)
        pl.semaphore_signal(barrier, inc=1, device_id=(g, zl * 8 + q), device_id_type=MESH)
    taps[c, y, zl, 0] = filt_a[...]
    taps[c, y, zl, 1] = filt_b[...]
    pl.semaphore_wait(barrier, 11)

    def copy(src, dst, send, recv, device):
        cp = pltpu.make_async_remote_copy(
            src_ref=src, dst_ref=dst, send_sem=send, recv_sem=recv, device_id=device, device_id_type=MESH
        )
        return cp

    sends = []

    def go(*args):
        cp = copy(*args)
        cp.start()
        sends.append(cp)

    for i, p in enumerate(zl_peers):
        mine = taps.at[c, y, zl]
        go(mine, mine, f1_send.at[i], f1_recv.at[zl], seq(p, y, c))
    for k, rows in enumerate((rows_b, rows_a)):
        go(rows.at[1:3, :, 128:256], halo.at[k], h_send.at[k], h_recv.at[k], (g, following))
    for p in zl_peers:
        got = taps.at[c, y, p]
        copy(got, got, f1_send.at[0], f1_recv.at[p], seq(p, y, c)).wait_recv()
    for i, p in enumerate(y_peers):
        mine = taps.at[c, y]
        go(mine, mine, f2_send.at[i], f2_recv.at[y], seq(zl, p, c))
    for p in y_peers:
        got = taps.at[c, p]
        copy(got, got, f2_send.at[0], f2_recv.at[p], seq(zl, p, c)).wait_recv()
    mine = taps.at[c]
    go(mine, mine, f3_send, f3_recv, seq(zl, y, 1 - c))
    got = taps.at[1 - c]
    copy(got, got, f3_send, f3_recv, seq(zl, y, 1 - c)).wait_recv()

    eye = eye_mask()
    has_halo = s > 0

    for ck, rows in ((1, rows_b), (0, rows_a)):
        k = 1 - ck
        copy(rows.at[1:3, :, 128:256], halo.at[k], h_send.at[k], h_recv.at[k], (g, following)).wait_recv()

        @pl.loop(0, CHAN // CHUNK)
        def _(i, ck=ck, k=k, rows=rows):
            at = pl.ds(pl.multiple_of(i * CHUNK, CHUNK), CHUNK)
            product = rows[1, at, :].astype(F32) * rows[2, at, :].astype(F32)
            before = halo[k, 0, at, :].astype(F32) * halo[k, 1, at, :].astype(F32)
            before = jnp.where(has_halo, before, 0.0)
            window = jnp.concatenate([before, product[:, :128]], axis=1)
            both = jnp.concatenate([window, product], axis=0)
            spectrum = dot3(both, wf_hi[...], wf_lo[...])
            f = jnp.concatenate([taps[d, b, i, ck] for b in range(4) for d in range(2)], axis=0)
            response = dot3(f, wf_hi[:128], wf_lo[:128])
            f_re, f_im = response[:, :128], response[:, 128:]
            parts = []
            for w in range(2):
                x_re = spectrum[w * CHUNK : (w + 1) * CHUNK, :128]
                x_im = spectrum[w * CHUNK : (w + 1) * CHUNK, 128:]
                parts.append(jnp.concatenate([x_re * f_re - x_im * f_im, x_re * f_im + x_im * f_re], axis=1))
            conv = dot3(jnp.concatenate(parts, axis=0), wi_hi[...], wi_lo[...])
            conv = jnp.concatenate([conv[:CHUNK], conv[CHUNK:]], axis=1)
            gated = rows[0, at, :].astype(F32) * conv
            average = jnp.sum(gated, axis=1, keepdims=True) * (1.0 / TOK)
            diff = gated - average
            squares = jnp.sum(diff * diff, axis=1, keepdims=True)
            centred[ck, at, :] = diff
            for h in range(CHUNK // 128):
                own[ck, 0, pl.ds(i * 2 + h, 1), :] = to_row(average[h * 128 : (h + 1) * 128], eye)
                own[ck, 1, pl.ds(i * 2 + h, 1), :] = to_row(squares[h * 128 : (h + 1) * 128], eye)

        level1[ck, y * 2 + c] = own[ck]
        for i in range(1, 8):
            q = lax.rem(y * 2 + c + i, 8)
            go(own.at[ck], level1.at[ck, y * 2 + c], s1_send.at[ck, i], s1_recv.at[ck, y * 2 + c], (g, zl * 8 + q))

    for ck, z in ((1, z_b), (0, z_a)):
        for i in range(1, 8):
            q = lax.rem(y * 2 + c + i, 8)
            copy(own.at[ck], level1.at[ck, q], s1_send.at[ck, i], s1_recv.at[ck, q], (g, zl * 8 + q)).wait_recv()
        mean1 = sum(level1[ck, q, 0] for q in range(8)) * 0.125
        square1 = sum(level1[ck, q, 1] for q in range(8))
        square1 = square1 + TOK * sum((level1[ck, q, 0] - mean1) * (level1[ck, q, 0] - mean1) for q in range(8))
        level2[ck, zl, 0] = mean1
        level2[ck, zl, 1] = square1
        for i, p in enumerate(zl_peers):
            mine = level2.at[ck, zl]
            go(mine, mine, s2_send.at[ck, i], s2_recv.at[ck, zl], seq(p, y, c))
    for ck, z in ((1, z_b), (0, z_a)):
        for p in zl_peers:
            got = level2.at[ck, p]
            copy(got, got, s2_send.at[ck, 0], s2_recv.at[ck, p], seq(p, y, c)).wait_recv()
        mean = sum(level2[ck, p, 0] for p in range(4)) * 0.25
        square = sum(level2[ck, p, 1] for p in range(4))
        square = square + 8 * TOK * sum((level2[ck, p, 0] - mean) * (level2[ck, p, 0] - mean) for p in range(4))
        scale = lax.rsqrt(square * (1.0 / TOKENS) + 1e-05)
        shift = own[ck, 0] - mean
        for j in range(8):
            at = slice(j * 128, (j + 1) * 128)
            shift_c = to_column(shift[j : j + 1], eye)
            scale_c = to_column(scale[j : j + 1], eye)
            z[at, :] = ((centred[ck, at, :] + shift_c) * scale_c).astype(BF)
    for cp in sends:
        cp.wait_send()


def back_kernel(
    z_a, z_b, out, alpha, beta, partial, landed,
    y_send, y_recv, a_send, a_recv, c_send, c_recv, z_send, z_recv, x_send, x_recv, o_send, o_recv, local,
):
    g, s, x, zh, zl, y, c = place()
    me = y * 2 + c
    barrier = pltpu.get_barrier_semaphore()
    x_peers = [lax.rem(x + i, 4) for i in range(1, 4)]
    y_peers = [lax.rem(y + i, 4) for i in range(1, 4)]
    other = (x * 2 + 1 - zh, s)

    @pl.loop(1, 32)
    def _(i):
        pl.semaphore_signal(barrier, inc=1, device_id=(g, lax.rem(s + i, 32)), device_id_type=MESH)

    for p in x_peers:
        pl.semaphore_signal(barrier, inc=1, device_id=(p * 2 + zh, s), device_id_type=MESH)
    pl.semaphore_signal(barrier, inc=1, device_id=other, device_id_type=MESH)
    pl.semaphore_wait(barrier, 35)

    def copy(src, dst, send, recv, device):
        return pltpu.make_async_remote_copy(
            src_ref=src, dst_ref=dst, send_sem=send, recv_sem=recv, device_id=device, device_id_type=MESH
        )

    sends = []

    def go(*args):
        cp = copy(*args)
        cp.start()
        sends.append(cp)

    def columns(q):
        return pl.ds(pl.multiple_of(q * TOK, TOK), TOK)

    def rows(q):
        return pl.ds(pl.multiple_of(q * 128, 128), 128)

    for i in range(1, 8):
        q = lax.rem(me + i, 8)
        go(z_b.at[rows(q)], beta.at[zh, x, :, columns(me)], y_send.at[i], y_recv.at[me], (g, zl * 8 + q))
    keep_b = pltpu.make_async_copy(z_b.at[rows(me)], beta.at[zh, x, :, columns(me)], local.at[0])
    keep_b.start()
    go(z_a, alpha.at[:, columns(me)], c_send.at[0], c_recv.at[y], (g, zl * 8 + y * 2 + 1 - c))
    for i, p in enumerate(y_peers):
        go(z_a, alpha.at[:, columns(me)], a_send.at[i], a_recv.at[y], (g, zl * 8 + p * 2 + c))
    keep_a = pltpu.make_async_copy(z_a, alpha.at[:, columns(me)], local.at[1])
    keep_a.start()
    keep_b.wait()
    for i in range(1, 8):
        q = lax.rem(me + i, 8)
        copy(z_b.at[rows(me)], beta.at[zh, x, :, columns(q)], y_send.at[i], y_recv.at[q], (g, zl * 8 + q)).wait_recv()
    panel = beta.at[zh, x]
    go(panel, panel, z_send, z_recv, other)
    for i, p in enumerate(x_peers):
        go(panel, panel, x_send.at[0, i], x_recv.at[0, x], (p * 2 + zh, s))
    for i, p in enumerate(y_peers):
        got = alpha.at[:, columns(p * 2 + c)]
        copy(z_a, got, a_send.at[i], a_recv.at[p], (g, zl * 8 + p * 2 + c)).wait_recv()
        go(got, got, c_send.at[1 + i], c_recv.at[p], (g, zl * 8 + y * 2 + 1 - c))
    far = beta.at[1 - zh, x]
    copy(far, far, z_send, z_recv, other).wait_recv()
    for i, p in enumerate(x_peers):
        go(far, far, x_send.at[1, i], x_recv.at[1, x], (p * 2 + zh, s))
    keep_a.wait()
    for p in range(4):
        got = alpha.at[:, columns(p * 2 + 1 - c)]
        copy(got, got, c_send.at[0], c_recv.at[p], (g, zl * 8 + y * 2 + 1 - c)).wait_recv()
    for half in range(2):
        zz = zh if half == 0 else 1 - zh
        for p in x_peers:
            got = beta.at[zz, p]
            copy(got, got, x_send.at[half, 0], x_recv.at[half, p], (p * 2 + zh, s)).wait_recv()

        @pl.loop(0, 4)
        def _(i, half=half, zz=zz):
            at = pl.ds(pl.multiple_of(i * 256, 256), 256)
            right = beta[zz].reshape(512, 8 * TOK)
            block = lax.dot_general(alpha[at, :], right, (((1,), (1,)), ((), ())), preferred_element_type=F32)
            partial[half, at, :] = (block * (1.0 / TOKENS)).astype(BF)

        landed[half, s] = partial[half, pl.ds(pl.multiple_of(s * 32, 32), 32), :]

        @pl.loop(1, 32)
        def _(i, half=half):
            t = lax.rem(s + i, 32)
            at = pl.ds(pl.multiple_of(t * 32, 32), 32)
            copy(partial.at[half, at], landed.at[half, s], o_send.at[half, i], o_recv.at[half, s], (g, t)).start()

    for half in range(2):
        zz = zh if half == 0 else 1 - zh

        @pl.loop(1, 32)
        def _(i, half=half):
            t = lax.rem(s + i, 32)
            at = pl.ds(pl.multiple_of(t * 32, 32), 32)
            copy(partial.at[half, at], landed.at[half, t], o_send.at[half, i], o_recv.at[half, t], (g, t)).wait_recv()

        @pl.loop(0, 8)
        def _(q, half=half, zz=zz):
            total = landed[half, q].astype(F32)
            for p in range(1, 4):
                total = total + landed[half, p * 8 + q].astype(F32)
            for p in range(4):
                at = pl.multiple_of((p * 2 + zz) * 1024 + q * 128, 128)
                out[:, pl.ds(at, 128)] = total[:, p * 128 : (p + 1) * 128]

    @pl.loop(1, 32)
    def _(i):
        for half in range(2):
            t = lax.rem(s + i, 32)
            at = pl.ds(pl.multiple_of(t * 32, 32), 32)
            copy(partial.at[half, at], landed.at[half, s], o_send.at[half, i], o_recv.at[half, s], (g, t)).wait_send()

    for cp in sends:
        cp.wait_send()


VMEM = pl.BlockSpec(memory_space=pltpu.VMEM)
DMA = pltpu.SemaphoreType.DMA


def front(rows_a, rows_b, filt_a, filt_b):
    consts = [jnp.asarray(w) for w in dft_constants()]
    return pl.pallas_call(
        front_kernel,
        out_shape=[jax.ShapeDtypeStruct((CHAN, TOK), BF)] * 2,
        in_specs=[VMEM] * 8,
        out_specs=[VMEM] * 2,
        scratch_shapes=[
            pltpu.VMEM((2, 2, CHAN, 128), BF),
            pltpu.VMEM((2, 4, 4, 2, 32, TAPS), F32),
            pltpu.VMEM((2, CHAN, TOK), F32),
            pltpu.VMEM((2, 2, 8, 128), F32),
            pltpu.VMEM((2, 8, 2, 8, 128), F32),
            pltpu.VMEM((2, 4, 2, 8, 128), F32),
            DMA((2,)), DMA((2,)), DMA((3,)), DMA((4,)), DMA((3,)), DMA((4,)), DMA, DMA,
            DMA((2, 8)), DMA((2, 8)), DMA((2, 3)), DMA((2, 4)),
        ],
        compiler_params=pltpu.CompilerParams(
            collective_id=0, has_side_effects=True, vmem_limit_bytes=56 * 2**20
        ),
        name="front",
    )(rows_a, rows_b, filt_a, filt_b, *consts)


def back(z_a, z_b):
    return pl.pallas_call(
        back_kernel,
        out_shape=jax.ShapeDtypeStruct((32, 8 * CHAN), F32),
        in_specs=[VMEM] * 2,
        out_specs=VMEM,
        scratch_shapes=[
            pltpu.VMEM((CHAN, 8 * TOK), BF),
            pltpu.VMEM((2, 4, 128, 8 * TOK), BF),
            pltpu.VMEM((2, CHAN, 512), BF),
            pltpu.VMEM((2, 32, 32, 512), BF),
            DMA((8,)), DMA((8,)), DMA((3,)), DMA((4,)), DMA((4,)), DMA((4,)), DMA, DMA,
            DMA((2, 3)), DMA((2, 4)), DMA((2, 32)), DMA((2, 32)), DMA((2,)),
        ],
        compiler_params=pltpu.CompilerParams(
            collective_id=1, has_side_effects=True, vmem_limit_bytes=56 * 2**20
        ),
        name="back",
    )(z_a, z_b)


def body(rows_alpha, rows_beta, filter_alpha, filter_beta):
    z_a, z_b = front(rows_alpha, rows_beta, filter_alpha, filter_beta)
    return back(z_a, z_b)


def solution(mesh):
    placed = (
        P(None, "grp", "seq"),
        P(None, "grp", "seq"),
        P(("grp", "seq"), None),
        P(("grp", "seq"), None),
    )
    return jax.shard_map(
        body, mesh=mesh, in_specs=placed, out_specs=P(("grp", "seq"), None), check_vma=False
    )
```

```python
import jax
import jax.numpy as jnp
import ml_dtypes
import numpy as np
from jax import lax
from jax.experimental import pallas as pl
from jax.experimental.pallas import tpu as pltpu
from jax.sharding import PartitionSpec as P

MESH = pl.DeviceIdType.MESH
BF = jnp.bfloat16
F32 = jnp.float32
TOKENS = 8192
CHAN = 1024
TOK = 256
TAPS = 128
CHUNK = 256


def split_const(matrix):
    high = matrix.astype(ml_dtypes.bfloat16)
    low = (matrix - high.astype(np.float64)).astype(ml_dtypes.bfloat16)
    return high, low


def dft_constants():
    n = np.arange(256)[:, None]
    k = np.arange(128)[None, :] + 0.5
    angle = 2.0 * np.pi * n * k / 256.0
    forward = np.concatenate([np.cos(angle), -np.sin(angle)], axis=1)
    back = angle[128:].T
    inverse = np.concatenate([np.cos(back), -np.sin(back)], axis=0) / 128.0
    return split_const(forward) + split_const(inverse)


def split(value):
    high = value.astype(BF)
    low = (value - high.astype(F32)).astype(BF)
    return high, low


def dot3(value, w_high, w_low):
    high, low = split(value)
    total = jnp.dot(low, w_high, preferred_element_type=F32)
    total = total + jnp.dot(high, w_low, preferred_element_type=F32)
    return total + jnp.dot(high, w_high, preferred_element_type=F32)


def place():
    g = lax.axis_index("grp")
    s = lax.axis_index("seq")
    return g, s, g // 2, g % 2, s // 8, (s // 2) % 4, s % 2


def eye_mask():
    r = lax.broadcasted_iota(jnp.int32, (128, 128), 0)
    c = lax.broadcasted_iota(jnp.int32, (128, 128), 1)
    return r == c


def to_row(column, eye):
    return jnp.sum(jnp.where(eye, jnp.broadcast_to(column, (128, 128)), 0.0), axis=0, keepdims=True)


def to_column(row, eye):
    return jnp.sum(jnp.where(eye, jnp.broadcast_to(row, (128, 128)), 0.0), axis=1, keepdims=True)


def kernel(
    all_a, all_b, filt_a, filt_b, wf_hi, wf_lo, wi_hi, wi_lo, out,
    kept, edge, halo, taps, centred, z_a, z_b, across, own, level1, level2, shifts, panel, pick, sums, alpha, beta,
    partial, exact, passed, landed,
    h_send, h_recv, f1_send, f1_recv, f2_send, f2_recv, f3_send, f3_recv, s1_send, s1_recv, s2_send, s2_recv,
    y_send, y_recv, w_send, w_recv, a_send, a_recv, c_send, c_recv, z_send, z_recv, x_send, x_recv, p_send, p_recv, r_send, r_recv, o_send, o_recv,
    local, l_sem,
):
    g, s, x, zh, zl, y, c = place()
    me = y * 2 + c
    zl_peers = [lax.rem(zl + i, 4) for i in range(1, 4)]
    y_peers = [lax.rem(y + i, 4) for i in range(1, 4)]
    x_peers = [lax.rem(x + i, 4) for i in range(1, 4)]
    sibling = (g, zl * 8 + y * 2 + 1 - c)
    other = (x * 2 + 1 - zh, s)

    side = zl // 2
    mate = side * 4 + 1 - zl
    outer = (zl + 1) % 4 < 2

    def chunk_at(k):
        far, near = 3 - 3 * side + (k % 2) * (2 * side - 1), mate + (k % 2) * (zl - mate)
        return (1 - k // 2) * far + (k // 2) * near

    def seq(a, b, d):
        return (g, a * 8 + b * 2 + d)

    barrier = pltpu.get_barrier_semaphore()

    def greet(device):
        pl.semaphore_signal(barrier, inc=1, device_id=device, device_id_type=MESH)

    @pl.loop(1, 32)
    def _(i):
        greet((g, lax.rem(s + i, 32)))

    for p in x_peers:
        greet((p * 2 + zh, s))
    greet(other)
    rows_a, rows_b = kept.at[0], kept.at[1]
    loads = []
    for ck, whole in ((1, all_b), (0, all_a)):
        for part in ((1, 3), (0, 1)):
            at = pl.ds(part[0], part[1] - part[0])
            load = pltpu.make_async_copy(whole.at[at], kept.at[ck, at], l_sem.at[ck, part[0]])
            load.start()
            loads.append(load)
    taps[0, c, y, zl] = filt_a[...]
    taps[1, c, y, zl] = filt_b[...]
    for ck in (1, 0):
        loads[2 - 2 * ck].wait()
        edge[ck] = (kept[ck, 1, :, 128:].astype(F32) * kept[ck, 2, :, 128:].astype(F32)).astype(BF)
    pl.semaphore_wait(barrier, 35)

    def copy(src, dst, send, recv, device):
        return pltpu.make_async_remote_copy(
            src_ref=src, dst_ref=dst, send_sem=send, recv_sem=recv, device_id=device, device_id_type=MESH
        )

    sends = []

    def go(*args):
        cp = copy(*args)
        cp.start()
        sends.append(cp)

    def arrive(dst, recv):
        copy(dst, dst, h_send.at[0], recv, sibling).wait_recv()

    def columns(q):
        return pl.ds(pl.multiple_of(q * TOK, TOK), TOK)

    def channels(q):
        return pl.ds(pl.multiple_of(q * 128, 128), 128)

    def chunk(i):
        return pl.ds(pl.multiple_of(i * CHUNK, CHUNK), CHUNK)

    def halo_out(ck):
        go(edge.at[ck], halo.at[ck], h_send.at[ck], h_recv.at[ck], (g, lax.rem(s + 1, 32)))

    def taps_copy(ck, i, p):
        mine = taps.at[ck, c, y]
        return copy(mine, mine, f2_send.at[ck, i], f2_recv.at[ck, y], seq(zl, p, c))

    for ck in (1, 0):
        for i, p in enumerate(zl_peers):
            mine = taps.at[ck, c, y, zl]
            go(mine, mine, f1_send.at[ck, i], f1_recv.at[ck, zl], seq(p, y, c))
        if ck == 1:
            halo_out(1)
    for ck in (1, 0):
        for p in zl_peers:
            arrive(taps.at[ck, c, y, p], f1_recv.at[ck, p])
        first = [taps_copy(ck, i, p) for i, p in enumerate(y_peers)]
        for cp in first:
            cp.start()
        if ck == 1:
            for cp in first:
                cp.wait_send()
            halo_out(0)
        else:
            sends.extend(first)

    lane = lax.broadcasted_iota(jnp.int32, (8 * TOK, 128), 1)
    slot = lax.broadcasted_iota(jnp.int32, (8 * TOK, 128), 0) // TOK
    pick[...] = jnp.where((lane < 24) & (lane % 8 == slot), 1.0, 0.0).astype(BF)

    eye = eye_mask()
    has_halo = s > 0

    def convolve(ck, rows, i):
        at = chunk(i)
        product = rows[1, at, :].astype(F32) * rows[2, at, :].astype(F32)
        before = jnp.where(has_halo, halo[ck, at, :].astype(F32), 0.0)
        window = jnp.concatenate([before, product[:, :128]], axis=1)
        spectrum = dot3(jnp.concatenate([window, product], axis=0), wf_hi[...], wf_lo[...])
        f = jnp.concatenate([taps[ck, d, b, i] for b in range(4) for d in range(2)], axis=0)
        response = dot3(f, wf_hi[:128], wf_lo[:128])
        f_re, f_im = response[:, :128], response[:, 128:]
        parts = []
        for w in range(2):
            x_re = spectrum[w * CHUNK : (w + 1) * CHUNK, :128]
            x_im = spectrum[w * CHUNK : (w + 1) * CHUNK, 128:]
            parts.append(jnp.concatenate([x_re * f_re - x_im * f_im, x_re * f_im + x_im * f_re], axis=1))
        conv = dot3(jnp.concatenate(parts, axis=0), wi_hi[...], wi_lo[...])
        conv = jnp.concatenate([conv[:CHUNK], conv[CHUNK:]], axis=1)
        gated = rows[0, at, :].astype(F32) * conv
        average = jnp.sum(gated, axis=1, keepdims=True) * (1.0 / TOK)
        diff = gated - average
        squares = jnp.sum(diff * diff, axis=1, keepdims=True)
        for h in range(CHUNK // 128):
            own[ck, 0, pl.ds(i * 2 + h, 1), :] = to_row(average[h * 128 : (h + 1) * 128], eye)
            own[ck, 1, pl.ds(i * 2 + h, 1), :] = to_row(squares[h * 128 : (h + 1) * 128], eye)
        return diff

    def to_sibling(ck):
        return copy(taps.at[ck, c], taps.at[ck, c], f3_send.at[ck], f3_recv.at[ck], sibling)

    def filters_half(ck):
        for p in y_peers:
            arrive(taps.at[ck, c, p], f2_recv.at[ck, p])
        to_sibling(ck).start()

    def filters_rest(ck):
        arrive(taps.at[ck, 1 - c], f3_recv.at[ck])
        arrive(halo.at[ck], h_recv.at[ck])

    def over_z(k):
        at = pl.ds(lax.rem(y + 1 + k, 4) * 2, 2)
        return copy(z_b.at[at], across.at[at], z_send.at[k], z_recv.at[k], other)

    def share(far, q):
        src, zz = (across, 1 - zh) if far else (z_b, zh)
        dst = beta.at[zz, columns(me), channels(x)]
        send, recv = (w_send, w_recv) if far else (y_send, y_recv)
        return copy(src.at[q], dst, send.at[q], recv.at[me], (g, zl * 8 + q))

    def relay_z(k):
        i = lax.rem(y + 1 + k, 4)
        arrive(across.at[pl.ds(i * 2, 2)], z_recv.at[k])
        for h in range(2):
            q = i * 2 + h

            @pl.when(q != me)
            def _(q=q):
                share(1, q).start()

    filters_half(1)
    filters_rest(1)
    loads[1].wait()

    @pl.loop(0, 4)
    def _(k):
        @pl.when(k == 2)
        def _():
            filters_half(0)

        i = lax.rem(y + 1 + k, 4)
        turned = convolve(1, rows_b, i).T.astype(BF)
        for h in range(2):
            z_b[i * 2 + h] = turned[:, h * 128 : (h + 1) * 128]
        over_z(k).start()
        for h in range(2):
            q = i * 2 + h

            @pl.when(q != me)
            def _(q=q):
                share(0, q).start()

    keep_b = pltpu.make_async_copy(z_b.at[me], beta.at[zh, columns(me), channels(x)], local.at[0])
    keep_b.start()

    filters_rest(0)
    loads[3].wait()

    @pl.loop(0, 4)
    def _(i):
        centred[chunk(i), :] = convolve(0, rows_a, i)

    level1[me] = own[...]
    for i in range(1, 8):
        q = lax.rem(me + i, 8)
        go(own, level1.at[me], s1_send.at[i], s1_recv.at[me], (g, zl * 8 + q))

    keep_b.wait()
    for i in range(1, 8):
        q = lax.rem(me + i, 8)
        arrive(beta.at[zh, columns(q), channels(x)], y_recv.at[q])
    up, down = (lax.rem(x + 1, 4) * 2 + zh, s), (lax.rem(x + 3, 4) * 2 + zh, s)

    def piece(far, step, part):
        zz = 1 - zh if far else zh
        return beta.at[zz, pl.ds(part * 1024, 1024), channels(lax.rem(x + step, 4))]

    def spread_x(far, part):
        src = piece(far, 0, part)
        for i, device in enumerate((up, down)):
            go(src, src, x_send.at[far, i, part], x_recv.at[far, 2 - 2 * i, part], device)

    def pass_on(far, part):
        src = piece(far, 3 - 2 * part, part)
        return copy(src, src, x_send.at[far, 2, part], x_recv.at[far, 1, part], down if part else up)

    def relay_x(far):
        for part in range(2):
            arrive(piece(far, 3 - 2 * part, part), x_recv.at[far, 2 - 2 * part, part])
            pass_on(far, part).start()

    def rest_x(far):
        for step, part in ((1, 0), (3, 1), (2, 0), (2, 1)):
            arrive(piece(far, step, part), x_recv.at[far, step - 1, part])

    for part in range(2):
        spread_x(0, part)

    for i in range(1, 8):
        q = lax.rem(me + i, 8)
        arrive(level1.at[q], s1_recv.at[q])
    for ck in range(2):
        mean1 = sum(level1[q, ck, 0] for q in range(8)) * 0.125
        square1 = sum(level1[q, ck, 1] for q in range(8))
        square1 = square1 + TOK * sum(
            (level1[q, ck, 0] - mean1) * (level1[q, ck, 0] - mean1) for q in range(8)
        )
        level2[zl, ck, 0] = mean1
        level2[zl, ck, 1] = square1
    for i, p in enumerate(zl_peers):
        go(level2.at[zl], level2.at[zl], s2_send.at[i], s2_recv.at[zl], seq(p, y, c))
    for p in zl_peers:
        arrive(level2.at[p], s2_recv.at[p])
    for ck in range(2):
        mean = sum(level2[p, ck, 0] for p in range(4)) * 0.25
        square = sum(level2[p, ck, 1] for p in range(4))
        square = square + 8 * TOK * sum(
            (level2[p, ck, 0] - mean) * (level2[p, ck, 0] - mean) for p in range(4)
        )
        scale = lax.rsqrt(square * (1.0 / TOKENS) + 1e-05)
        shifts[ck, 0] = own[0, 0] - mean if ck == 0 else mean
        shifts[ck, 1] = scale

    def alpha_out(k):
        at = chunk(chunk_at(k))
        src, dst = z_a.at[at], alpha.at[at, columns(me)]
        for j, p in enumerate(y_peers):
            go(src, dst, a_send.at[k, j], a_recv.at[k, y], seq(zl, p, c))
        go(src, dst, c_send.at[k, y], c_recv.at[k, y], sibling)

    for k in range(4):
        for h in range(2):
            block = chunk_at(k) * 2 + h
            shift_c = to_column(shifts[0, 0, pl.ds(block, 1), :], eye)
            scale_c = to_column(shifts[0, 1, pl.ds(block, 1), :], eye)
            z_a[channels(block), :] = ((centred[channels(block), :] + shift_c) * scale_c).astype(BF)
        if k < 2:
            alpha_out(k)
    keep_a = pltpu.make_async_copy(z_a, alpha.at[:, columns(me)], local.at[1])
    keep_a.start()

    mean_b = shifts[1, 0, pl.ds(me, 1), :]
    for q in range(8):
        panel[zh, x, q : q + 1, :] = level1[q, 1, 0, pl.ds(me, 1), :] - mean_b
    panel[zh, x, 8:9, :] = shifts[1, 1, pl.ds(me, 1), :]
    panel[zh, x, 9:16, :] = jnp.zeros((7, 128), F32)
    mine = panel.at[zh, x]
    go(mine, mine, p_send.at[6], p_recv.at[1, x], other)
    for i, p in enumerate(x_peers):
        go(mine, mine, p_send.at[i], p_recv.at[0, x], (p * 2 + zh, s))

    def alpha_slot(k, p, d):
        return alpha.at[chunk(chunk_at(k)), columns(p * 2 + d)]

    def alpha_copy(k, p):
        got = alpha_slot(k, p, c)
        return copy(got, got, c_send.at[k, p], c_recv.at[k, p], sibling)

    def relay_alpha(k):
        for p in y_peers:
            arrive(alpha_slot(k, p, c), a_recv.at[k, p])
            alpha_copy(k, p).start()

    relay_x(0)
    for k in range(4):
        relay_z(k)
    keep_f = pltpu.make_async_copy(across.at[me], beta.at[1 - zh, columns(me), channels(x)], local.at[0])
    keep_f.start()
    relay_alpha(0)
    keep_f.wait()
    for i in range(1, 8):
        q = lax.rem(me + i, 8)
        arrive(beta.at[1 - zh, columns(q), channels(x)], w_recv.at[q])
    for part in range(2):
        spread_x(1, part)
    alpha_out(2)
    alpha_out(3)
    relay_alpha(1)
    mine = panel.at[1 - zh, x]
    arrive(mine, p_recv.at[1, x])
    for i, p in enumerate(x_peers):
        go(mine, mine, p_send.at[3 + i], p_recv.at[2, x], (p * 2 + zh, s))
    keep_a.wait()

    lane = lax.broadcasted_iota(jnp.int32, (CHUNK, 128), 1)
    low_lanes = (lane >= 8) & (lane < 16)

    def hand(half, k):
        return copy(
            partial.at[half, chunk(chunk_at(k))], passed.at[half, k], r_send.at[half, k], r_recv.at[half, k],
            (g, mate * 8 + me),
        )

    def deliver(half, k, q):
        i = chunk_at(k)
        src = partial.at[half, pl.ds(pl.multiple_of((i * 8 + q) * 32, 32), 32)]
        kind = 2 * (1 - k // 2) + (k // 2) * (1 - k % 2)
        return copy(src, landed.at[half, kind, me], o_send.at[half, k, q], o_recv.at[half, kind, me], (g, i * 8 + q))

    def deliver_all(half, k):
        @pl.loop(0, 8)
        def _(j):
            deliver(half, k, lax.rem(me + j, 8)).start()

    def join(half, k):
        @pl.when(jnp.logical_not(outer))
        def _():
            arrive(passed.at[half, k], r_recv.at[half, k])
            at = chunk(chunk_at(k))
            partial[half, at, :] = (exact[k] + passed[half, k].astype(F32)).astype(BF)
            deliver_all(half, k)

    for half in range(2):
        zz = zh if half == 0 else 1 - zh
        rest_x(half)
        for p in x_peers:
            arrive(panel.at[zz, p], p_recv.at[2 * half, p])
        delta = jnp.concatenate([panel[zz, p, 0:8, :] for p in range(4)], axis=1)
        weight = jnp.concatenate([panel[zz, p, 8:9, :] for p in range(4)], axis=1) * (1.0 / TOKENS)
        delta_hi = delta.astype(BF).astype(F32)
        spread = jnp.concatenate(
            [delta_hi, delta_hi, delta - delta_hi, jnp.zeros((104, 512), F32)], axis=0
        ).astype(BF)

        @pl.loop(0, 4)
        def _(k, half=half, zz=zz, spread=spread, weight=weight):
            at = chunk(chunk_at(k))

            @pl.when(k >= 2)
            def _():
                join(half, k - 2)

            if half == 0:
                for p in range(4):
                    arrive(alpha_slot(k, p, 1 - c), c_recv.at[k, p])
                total = jnp.dot(alpha[at, :], pick[...], preferred_element_type=F32)
                total_hi = total.astype(BF).astype(F32)
                sums[at, :] = jnp.where(low_lanes, total - total_hi, total_hi).astype(BF)
            block = jnp.dot(alpha[at, :], beta[zz], preferred_element_type=F32)
            block = block + jnp.dot(sums[at, :], spread, preferred_element_type=F32)
            block = block * weight
            partial[half, at, :] = block.astype(BF)

            @pl.when(k < 2)
            def _():
                exact[k] = block

                @pl.when(outer)
                def _():
                    hand(half, k).start()

                if half == 0:
                    relay_alpha(k + 2)

                    @pl.when(k == 1)
                    def _():
                        relay_x(1)

            @pl.when(k == 2)
            def _():
                deliver_all(half, 2)

        @pl.loop(1, 8)
        def _(j, half=half):
            deliver(half, 3, lax.rem(me + j, 8)).start()

        landed[half, 0, me] = partial[half, pl.ds(pl.multiple_of(s * 32, 32), 32), :]

    for half in range(2):
        zz = zh if half == 0 else 1 - zh

        @pl.loop(1, 8)
        def _(j, half=half):
            q = lax.rem(me + j, 8)
            arrive(landed.at[half, 0, q], o_recv.at[half, 0, q])

        @pl.loop(0, 8)
        def _(q, half=half, zz=zz):
            for kind in (1, 2):
                arrive(landed.at[half, kind, q], o_recv.at[half, kind, q])
            total = landed[half, 0, q].astype(F32) + landed[half, 1, q].astype(F32)
            total = total + landed[half, 2, q].astype(F32)
            for p in range(4):
                at = pl.multiple_of((p * 2 + zz) * 1024 + q * 128, 128)
                out[:, pl.ds(at, 128)] = total[:, p * 128 : (p + 1) * 128]

    for half in range(2):
        for k in range(4):

            @pl.loop(1 if k == 3 else 0, 8)
            def _(j, half=half, k=k):
                @pl.when(jnp.logical_not(outer) | (k >= 2))
                def _():
                    deliver(half, k, lax.rem(me + j, 8)).wait_send()

        @pl.when(outer)
        def _(half=half):
            for k in range(2):
                hand(half, k).wait_send()

    @pl.loop(1, 8)
    def _(i):
        q = lax.rem(me + i, 8)
        share(0, q).wait_send()
        share(1, q).wait_send()

    for k in range(4):
        over_z(k).wait_send()
    for far in range(2):
        for part in range(2):
            pass_on(far, part).wait_send()
    for ck in range(2):
        to_sibling(ck).wait_send()
    for k in range(4):
        for p in y_peers:
            alpha_copy(k, p).wait_send()
    for cp in sends:
        cp.wait_send()


VMEM = pl.BlockSpec(memory_space=pltpu.VMEM)
DMA = pltpu.SemaphoreType.DMA


def body(rows_alpha, rows_beta, filter_alpha, filter_beta):
    consts = [jnp.asarray(w) for w in dft_constants()]
    return pl.pallas_call(
        kernel,
        out_shape=jax.ShapeDtypeStruct((32, 8 * CHAN), F32),
        in_specs=[pl.BlockSpec(memory_space=pl.ANY)] * 2 + [VMEM] * 6,
        out_specs=VMEM,
        scratch_shapes=[
            pltpu.VMEM((2, 3, CHAN, TOK), BF),
            pltpu.VMEM((2, CHAN, 128), BF),
            pltpu.VMEM((2, CHAN, 128), BF),
            pltpu.VMEM((2, 2, 4, 4, 32, TAPS), F32),
            pltpu.VMEM((CHAN, TOK), F32),
            pltpu.VMEM((CHAN, TOK), BF),
            pltpu.VMEM((8, TOK, 128), BF),
            pltpu.VMEM((8, TOK, 128), BF),
            pltpu.VMEM((2, 2, 8, 128), F32),
            pltpu.VMEM((8, 2, 2, 8, 128), F32),
            pltpu.VMEM((4, 2, 2, 8, 128), F32),
            pltpu.VMEM((2, 2, 8, 128), F32),
            pltpu.VMEM((2, 4, 16, 128), F32),
            pltpu.VMEM((8 * TOK, 128), BF),
            pltpu.VMEM((CHAN, 128), BF),
            pltpu.VMEM((CHAN, 8 * TOK), BF),
            pltpu.VMEM((2, 8 * TOK, 512), BF),
            pltpu.VMEM((2, CHAN, 512), BF),
            pltpu.VMEM((2, CHUNK, 512), F32),
            pltpu.VMEM((2, 2, CHUNK, 512), BF),
            pltpu.VMEM((2, 3, 8, 32, 512), BF),
            DMA((2,)), DMA((2,)), DMA((2, 3)), DMA((2, 4)), DMA((2, 3)), DMA((2, 4)), DMA((2,)), DMA((2,)),
            DMA((8,)), DMA((8,)), DMA((3,)), DMA((4,)),
            DMA((8,)), DMA((8,)), DMA((8,)), DMA((8,)), DMA((4, 3)), DMA((4, 4)), DMA((4, 4)), DMA((4, 4)),
            DMA((4,)), DMA((4,)), DMA((2, 3, 2)), DMA((2, 3, 2)), DMA((7,)), DMA((3, 4)), DMA((2, 2)), DMA((2, 2)),
            DMA((2, 4, 8)), DMA((2, 3, 8)), DMA((2,)), DMA((2, 2)),
        ],
        compiler_params=pltpu.CompilerParams(
            collective_id=0, has_side_effects=True, vmem_limit_bytes=56 * 2**20
        ),
        name="correlate",
    )(rows_alpha, rows_beta, filter_alpha, filter_beta, *consts)


def solution(mesh):
    placed = (
        P(None, "grp", "seq"),
        P(None, "grp", "seq"),
        P(("grp", "seq"), None),
        P(("grp", "seq"), None),
    )
    return jax.shard_map(
        body, mesh=mesh, in_specs=placed, out_specs=P(("grp", "seq"), None), check_vma=False
    )
```

```python
import jax
import jax.numpy as jnp
import ml_dtypes
import numpy as np
from jax import lax
from jax.experimental import pallas as pl
from jax.experimental.pallas import tpu as pltpu
from jax.sharding import PartitionSpec as P

MESH = pl.DeviceIdType.MESH
BF = jnp.bfloat16
F32 = jnp.float32
TOKENS = 8192
CHAN = 1024
TOK = 256
TAPS = 128
CHUNK = 256


def split_const(matrix):
    high = matrix.astype(ml_dtypes.bfloat16)
    low = (matrix - high.astype(np.float64)).astype(ml_dtypes.bfloat16)
    return high, low


def dft_constants():
    n = np.arange(256)[:, None]
    k = np.arange(128)[None, :] + 0.5
    angle = 2.0 * np.pi * n * k / 256.0
    forward = np.concatenate([np.cos(angle), -np.sin(angle)], axis=1)
    back = angle[128:].T
    inverse = np.concatenate([np.cos(back), -np.sin(back)], axis=0) / 128.0
    return split_const(forward) + split_const(inverse)


def split(value):
    high = value.astype(BF)
    low = (value - high.astype(F32)).astype(BF)
    return high, low


def dot3(value, w_high, w_low):
    high, low = split(value)
    total = jnp.dot(low, w_high, preferred_element_type=F32)
    total = total + jnp.dot(high, w_low, preferred_element_type=F32)
    return total + jnp.dot(high, w_high, preferred_element_type=F32)


def place():
    g = lax.axis_index("grp")
    s = lax.axis_index("seq")
    return g, s, g // 2, g % 2, s // 8, (s // 2) % 4, s % 2


def eye_mask():
    r = lax.broadcasted_iota(jnp.int32, (128, 128), 0)
    c = lax.broadcasted_iota(jnp.int32, (128, 128), 1)
    return r == c


def to_row(column, eye):
    return jnp.sum(jnp.where(eye, jnp.broadcast_to(column, (128, 128)), 0.0), axis=0, keepdims=True)


def to_column(row, eye):
    return jnp.sum(jnp.where(eye, jnp.broadcast_to(row, (128, 128)), 0.0), axis=1, keepdims=True)


def kernel(
    all_a, all_b, filt_a, filt_b, wf_hi, wf_lo, wi_hi, wi_lo, out,
    kept, edge, halo, taps, centred, z_a, z_b, across, own, level1, level2, shifts, panel, pick, sums, alpha, beta,
    partial, exact, passed, landed,
    h_send, h_recv, f1_send, f1_recv, f2_send, f2_recv, f3_send, f3_recv, s1_send, s1_recv, s2_send, s2_recv,
    y_send, y_recv, w_send, w_recv, a_send, a_recv, c_send, c_recv, z_send, z_recv, x_send, x_recv, p_send, p_recv, r_send, r_recv, o_send, o_recv,
    local, l_sem,
):
    g, s, x, zh, zl, y, c = place()
    me = y * 2 + c
    zl_peers = [lax.rem(zl + i, 4) for i in range(1, 4)]
    y_peers = [lax.rem(y + i, 4) for i in range(1, 4)]
    x_peers = [lax.rem(x + i, 4) for i in range(1, 4)]
    sibling = (g, zl * 8 + y * 2 + 1 - c)
    other = (x * 2 + 1 - zh, s)

    side = zl // 2
    mate = side * 4 + 1 - zl
    outer = (zl + 1) % 4 < 2

    def chunk_at(k):
        far, near = 3 - 3 * side + (k % 2) * (2 * side - 1), mate + (k % 2) * (zl - mate)
        return (1 - k // 2) * far + (k // 2) * near

    def seq(a, b, d):
        return (g, a * 8 + b * 2 + d)

    barrier = pltpu.get_barrier_semaphore()

    def greet(device):
        pl.semaphore_signal(barrier, inc=1, device_id=device, device_id_type=MESH)

    @pl.loop(1, 32)
    def _(i):
        greet((g, lax.rem(s + i, 32)))

    for p in x_peers:
        greet((p * 2 + zh, s))
    greet(other)
    rows_a, rows_b = kept.at[0], kept.at[1]
    loads = []
    for ck, whole in ((0, all_a), (1, all_b)):
        for part in ((1, 3), (0, 1)):
            at = pl.ds(part[0], part[1] - part[0])
            load = pltpu.make_async_copy(whole.at[at], kept.at[ck, at], l_sem.at[ck, part[0]])
            load.start()
            loads.append(load)
    taps[0, c, y, zl] = filt_a[...]
    taps[1, c, y, zl] = filt_b[...]
    for ck in range(2):
        loads[2 * ck].wait()
        edge[ck] = (kept[ck, 1, :, 128:].astype(F32) * kept[ck, 2, :, 128:].astype(F32)).astype(BF)
    pl.semaphore_wait(barrier, 35)

    def copy(src, dst, send, recv, device):
        return pltpu.make_async_remote_copy(
            src_ref=src, dst_ref=dst, send_sem=send, recv_sem=recv, device_id=device, device_id_type=MESH
        )

    sends = []

    def go(*args):
        cp = copy(*args)
        cp.start()
        sends.append(cp)

    def arrive(dst, recv):
        copy(dst, dst, h_send.at[0], recv, sibling).wait_recv()

    def columns(q):
        return pl.ds(pl.multiple_of(q * TOK, TOK), TOK)

    def channels(q):
        return pl.ds(pl.multiple_of(q * 128, 128), 128)

    def chunk(i):
        return pl.ds(pl.multiple_of(i * CHUNK, CHUNK), CHUNK)

    def halo_out(ck):
        go(edge.at[ck], halo.at[ck], h_send.at[ck], h_recv.at[ck], (g, lax.rem(s + 1, 32)))

    def taps_copy(ck, i, p):
        mine = taps.at[ck, c, y]
        return copy(mine, mine, f2_send.at[ck, i], f2_recv.at[ck, y], seq(zl, p, c))

    for ck in range(2):
        for i, p in enumerate(zl_peers):
            mine = taps.at[ck, c, y, zl]
            go(mine, mine, f1_send.at[ck, i], f1_recv.at[ck, zl], seq(p, y, c))
    for ck in range(2):
        halo_out(ck)
    for ck in range(2):
        for p in zl_peers:
            arrive(taps.at[ck, c, y, p], f1_recv.at[ck, p])
        first = [taps_copy(ck, i, p) for i, p in enumerate(y_peers)]
        for cp in first:
            cp.start()
        if ck == 0:
            for cp in first:
                cp.wait_send()
        else:
            sends.extend(first)

    lane = lax.broadcasted_iota(jnp.int32, (8 * TOK, 128), 1)
    slot = lax.broadcasted_iota(jnp.int32, (8 * TOK, 128), 0) // TOK
    pick[...] = jnp.where((lane < 24) & (lane % 8 == slot), 1.0, 0.0).astype(BF)

    eye = eye_mask()
    has_halo = s > 0

    def convolve(ck, rows, i):
        at = chunk(i)
        product = rows[1, at, :].astype(F32) * rows[2, at, :].astype(F32)
        before = jnp.where(has_halo, halo[ck, at, :].astype(F32), 0.0)
        window = jnp.concatenate([before, product[:, :128]], axis=1)
        spectrum = dot3(jnp.concatenate([window, product], axis=0), wf_hi[...], wf_lo[...])
        f = jnp.concatenate([taps[ck, d, b, i] for b in range(4) for d in range(2)], axis=0)
        response = dot3(f, wf_hi[:128], wf_lo[:128])
        f_re, f_im = response[:, :128], response[:, 128:]
        parts = []
        for w in range(2):
            x_re = spectrum[w * CHUNK : (w + 1) * CHUNK, :128]
            x_im = spectrum[w * CHUNK : (w + 1) * CHUNK, 128:]
            parts.append(jnp.concatenate([x_re * f_re - x_im * f_im, x_re * f_im + x_im * f_re], axis=1))
        conv = dot3(jnp.concatenate(parts, axis=0), wi_hi[...], wi_lo[...])
        conv = jnp.concatenate([conv[:CHUNK], conv[CHUNK:]], axis=1)
        gated = rows[0, at, :].astype(F32) * conv
        average = jnp.sum(gated, axis=1, keepdims=True) * (1.0 / TOK)
        diff = gated - average
        squares = jnp.sum(diff * diff, axis=1, keepdims=True)
        for h in range(CHUNK // 128):
            own[ck, 0, pl.ds(i * 2 + h, 1), :] = to_row(average[h * 128 : (h + 1) * 128], eye)
            own[ck, 1, pl.ds(i * 2 + h, 1), :] = to_row(squares[h * 128 : (h + 1) * 128], eye)
        return diff

    def to_sibling(ck):
        return copy(taps.at[ck, c], taps.at[ck, c], f3_send.at[ck], f3_recv.at[ck], sibling)

    def filters_half(ck):
        for p in y_peers:
            arrive(taps.at[ck, c, p], f2_recv.at[ck, p])
        to_sibling(ck).start()

    def filters_rest(ck):
        arrive(taps.at[ck, 1 - c], f3_recv.at[ck])
        arrive(halo.at[ck], h_recv.at[ck])

    def over_z(part, k):
        at = pl.ds(lax.rem(y + 1 + k, 4) * 2, 2)
        return copy(z_b.at[part, at], across.at[part, at], z_send.at[part, k], z_recv.at[part, k], other)

    def share_near(q):
        dst = beta.at[zh, me, :, :, channels(x)]
        return copy(z_b.at[:, q], dst, y_send.at[q], y_recv.at[me], (g, zl * 8 + q))

    def share_far(part, q):
        dst = beta.at[1 - zh, me, part, :, channels(x)]
        return copy(across.at[part, q], dst, w_send.at[part, q], w_recv.at[part, me], (g, zl * 8 + q))

    def relay_z(part):
        for k in range(4):
            i = lax.rem(y + 1 + k, 4)
            arrive(across.at[part, pl.ds(i * 2, 2)], z_recv.at[part, k])
            for h in range(2):
                q = i * 2 + h

                @pl.when(q != me)
                def _(q=q):
                    share_far(part, q).start()

        keep = pltpu.make_async_copy(across.at[part, me], beta.at[1 - zh, me, part, :, channels(x)], local.at[0])
        keep.start()
        keep.wait()

    up, down = (lax.rem(x + 1, 4) * 2 + zh, s), (lax.rem(x + 3, 4) * 2 + zh, s)

    def piece(far, step, part, at=slice(None)):
        zz = 1 - zh if far else zh
        return beta.at[zz, at, part, :, channels(lax.rem(x + step, 4))]

    def spread_x(far, part):
        src = piece(far, 0, part)
        for i, device in enumerate((up, down)):
            go(src, src, x_send.at[far, i, part, 0], x_recv.at[far, 2 - 2 * i, part, 0], device)

    def pass_on(far, part, i):
        src = piece(far, 3 - 2 * i, part, pl.ds(4 * i, 4))
        return copy(src, src, x_send.at[far, i, part, 1], x_recv.at[far, 1, part, i], down if i else up)

    def relay_x(far, part):
        for i in range(2):
            arrive(piece(far, 3 - 2 * i, part), x_recv.at[far, 2 - 2 * i, part, 0])
            pass_on(far, part, i).start()

    def rest_x(far):
        for part in range(2):
            for i in range(2):
                arrive(piece(far, 2, part, pl.ds(4 * i, 4)), x_recv.at[far, 1, part, i])

    def level_z(ck):
        level1[zl, ck] = own[ck]
        for i, p in enumerate(zl_peers):
            go(own.at[ck], level1.at[zl, ck], s1_send.at[ck, i], s1_recv.at[ck, zl], seq(p, y, c))

    def merge(parts, count):
        mean = sum(m for m, _ in parts) * (1.0 / len(parts))
        square = sum(v for _, v in parts)
        return mean, square + count * sum((m - mean) * (m - mean) for m, _ in parts)

    def level_y(ck):
        for p in zl_peers:
            arrive(level1.at[p, ck], s1_recv.at[ck, p])
        mean, square = merge([(level1[p, ck, 0], level1[p, ck, 1]) for p in range(4)], TOK)
        level2[me, ck, 0] = mean
        level2[me, ck, 1] = square
        level2[me, ck, 2] = own[ck, 0]
        for i in range(1, 8):
            q = lax.rem(me + i, 8)
            mine = level2.at[me, ck]
            go(mine, mine, s2_send.at[ck, i], s2_recv.at[ck, me], (g, zl * 8 + q))

    def statistics(ck):
        for i in range(1, 8):
            q = lax.rem(me + i, 8)
            arrive(level2.at[q, ck], s2_recv.at[ck, q])
        mean, square = merge([(level2[q, ck, 0], level2[q, ck, 1]) for q in range(8)], 4 * TOK)
        shifts[ck, 0] = own[ck, 0] - mean if ck == 0 else mean
        shifts[ck, 1] = lax.rsqrt(square * (1.0 / TOKENS) + 1e-05)

    filters_half(0)
    filters_rest(0)
    loads[1].wait()

    @pl.loop(0, 4)
    def _(i):
        centred[chunk(i), :] = convolve(0, rows_a, i)

    level_z(0)
    filters_half(1)
    level_y(0)

    filters_rest(1)
    loads[3].wait()

    @pl.loop(0, 4)
    def _(k):
        i = lax.rem(y + 1 + k, 4)
        turned = convolve(1, rows_b, i).T.astype(BF)
        for h in range(2):
            for part in range(2):
                z_b[part, i * 2 + h] = turned[part * 128 : (part + 1) * 128, h * 128 : (h + 1) * 128]
        for h in range(2):
            q = i * 2 + h

            @pl.when(q != me)
            def _(q=q):
                share_near(q).start()

    keep_b = pltpu.make_async_copy(z_b.at[:, me], beta.at[zh, me, :, :, channels(x)], local.at[0])
    keep_b.start()
    level_z(1)
    statistics(0)

    def alpha_out(k):
        at = chunk(chunk_at(k))
        src, dst = z_a.at[at], alpha.at[at, columns(me)]
        for j, p in enumerate(y_peers):
            go(src, dst, a_send.at[k, j], a_recv.at[k, y], seq(zl, p, c))
        go(src, dst, c_send.at[k, y], c_recv.at[k, y], sibling)

    for k in range(4):
        for h in range(2):
            block = chunk_at(k) * 2 + h
            shift_c = to_column(shifts[0, 0, pl.ds(block, 1), :], eye)
            scale_c = to_column(shifts[0, 1, pl.ds(block, 1), :], eye)
            z_a[channels(block), :] = ((centred[channels(block), :] + shift_c) * scale_c).astype(BF)
    level_y(1)
    for k in range(4):
        over_z(0, k).start()
    alpha_out(0)
    alpha_out(1)
    keep_a = pltpu.make_async_copy(z_a, alpha.at[:, columns(me)], local.at[1])
    keep_a.start()

    keep_b.wait()
    for i in range(1, 8):
        q = lax.rem(me + i, 8)
        arrive(beta.at[zh, q, :, :, channels(x)], y_recv.at[q])
    for part in range(2):
        spread_x(0, part)
    alpha_out(2)
    relay_x(0, 0)
    for k in range(4):
        over_z(1, k).start()
    statistics(1)

    mean_b = shifts[1, 0, pl.ds(me, 1), :]
    for q in range(8):
        panel[zh, x, q : q + 1, :] = level2[q, 1, 2, pl.ds(me, 1), :] - mean_b
    panel[zh, x, 8:9, :] = shifts[1, 1, pl.ds(me, 1), :]
    panel[zh, x, 9:16, :] = jnp.zeros((7, 128), F32)
    mine = panel.at[zh, x]
    go(mine, mine, p_send.at[6], p_recv.at[1, x], other)
    for i, p in enumerate(x_peers):
        go(mine, mine, p_send.at[i], p_recv.at[0, x], (p * 2 + zh, s))

    def alpha_slot(k, p, d):
        return alpha.at[chunk(chunk_at(k)), columns(p * 2 + d)]

    def alpha_copy(k, p):
        got = alpha_slot(k, p, c)
        return copy(got, got, c_send.at[k, p], c_recv.at[k, p], sibling)

    def relay_alpha(k):
        for p in y_peers:
            arrive(alpha_slot(k, p, c), a_recv.at[k, p])
            alpha_copy(k, p).start()

    def far_in(part):
        for i in range(1, 8):
            q = lax.rem(me + i, 8)
            arrive(beta.at[1 - zh, q, part, :, channels(x)], w_recv.at[part, q])
        spread_x(1, part)

    relay_z(0)
    alpha_out(3)
    relay_x(0, 1)
    far_in(0)
    relay_alpha(0)
    relay_alpha(1)
    relay_z(1)
    relay_alpha(2)
    keep_a.wait()

    lane = lax.broadcasted_iota(jnp.int32, (CHUNK, 128), 1)
    low_lanes = (lane >= 8) & (lane < 16)

    def hand(half, k, part):
        rows = pl.ds(pl.multiple_of(chunk_at(k) * CHUNK + part * 128, 128), 128)
        return copy(
            partial.at[half, rows], passed.at[half, k, pl.ds(part * 128, 128)],
            r_send.at[half, k, part], r_recv.at[half, k, part], (g, mate * 8 + me),
        )

    def deliver(half, k, q):
        i = chunk_at(k)
        src = partial.at[half, pl.ds(pl.multiple_of((i * 8 + q) * 32, 32), 32)]
        kind = 2 * (1 - k // 2) + (k // 2) * (1 - k % 2)
        return copy(src, landed.at[half, kind, me], o_send.at[half, k, q], o_recv.at[half, kind, me], (g, i * 8 + q))

    def deliver_all(half, k):
        @pl.loop(0, 8)
        def _(j):
            deliver(half, k, lax.rem(me + j, 8)).start()

    def join(half, k):
        @pl.when(jnp.logical_not(outer))
        def _():
            for part in range(2):
                rows = pl.ds(part * 128, 128)
                arrive(passed.at[half, k, rows], r_recv.at[half, k, part])
                at = pl.ds(pl.multiple_of(chunk_at(k) * CHUNK + part * 128, 128), 128)
                partial[half, at, :] = (exact[k, rows, :] + passed[half, k, rows, :].astype(F32)).astype(BF)

                @pl.loop(0, 4)
                def _(j, part=part):
                    deliver(half, k, part * 4 + lax.rem(me + j, 4)).start()

    def columns_in(half):
        zz = zh if half == 0 else 1 - zh
        rest_x(half)
        for p in x_peers:
            arrive(panel.at[zz, p], p_recv.at[2 * half, p])
        delta = jnp.concatenate([panel[zz, p, 0:8, :] for p in range(4)], axis=1)
        weight = jnp.concatenate([panel[zz, p, 8:9, :] for p in range(4)], axis=1) * (1.0 / TOKENS)
        delta_hi = delta.astype(BF).astype(F32)
        spread = jnp.concatenate(
            [delta_hi, delta_hi, delta - delta_hi, jnp.zeros((104, 512), F32)], axis=0
        ).astype(BF)
        return zz, spread, weight

    def product(half, first, last, found):
        zz, spread, weight = found

        @pl.loop(first, last)
        def _(k):
            at = chunk(chunk_at(k))
            if half == 0:
                for p in range(4):
                    arrive(alpha_slot(k, p, 1 - c), c_recv.at[k, p])
                total = jnp.dot(alpha[at, :], pick[...], preferred_element_type=F32)
                total_hi = total.astype(BF).astype(F32)
                sums[at, :] = jnp.where(low_lanes, total - total_hi, total_hi).astype(BF)
            block = jnp.dot(alpha[at, :], beta[zz].reshape(8 * TOK, 512), preferred_element_type=F32)
            block = block + jnp.dot(sums[at, :], spread, preferred_element_type=F32)
            block = block * weight
            partial[half, at, :] = block.astype(BF)
            if first < 2:
                exact[k] = block

                @pl.when(outer)
                def _():
                    for part in range(2):
                        hand(half, k, part).start()

            else:

                @pl.when(k == 2)
                def _():
                    deliver_all(half, 2)

        if last == 4:

            @pl.loop(1, 8)
            def _(j):
                deliver(half, 3, lax.rem(me + j, 8)).start()

            landed[half, 0, me] = partial[half, pl.ds(pl.multiple_of(s * 32, 32), 32), :]

    found = columns_in(0)
    product(0, 0, 2, found)
    far_in(1)
    mine = panel.at[1 - zh, x]
    arrive(mine, p_recv.at[1, x])
    for i, p in enumerate(x_peers):
        go(mine, mine, p_send.at[3 + i], p_recv.at[2, x], (p * 2 + zh, s))
    relay_alpha(3)
    relay_x(1, 0)
    product(0, 2, 4, found)
    join(0, 0)
    relay_x(1, 1)
    join(0, 1)
    found = columns_in(1)
    product(1, 0, 2, found)
    product(1, 2, 4, found)
    join(1, 0)
    join(1, 1)

    for half in range(2):
        zz = zh if half == 0 else 1 - zh

        @pl.loop(1, 8)
        def _(j, half=half):
            q = lax.rem(me + j, 8)
            arrive(landed.at[half, 0, q], o_recv.at[half, 0, q])

        @pl.loop(0, 8)
        def _(q, half=half, zz=zz):
            for kind in (1, 2):
                arrive(landed.at[half, kind, q], o_recv.at[half, kind, q])
            total = landed[half, 0, q].astype(F32) + landed[half, 1, q].astype(F32)
            total = total + landed[half, 2, q].astype(F32)
            for p in range(4):
                at = pl.multiple_of((p * 2 + zz) * 1024 + q * 128, 128)
                out[:, pl.ds(at, 128)] = total[:, p * 128 : (p + 1) * 128]

    for half in range(2):
        for k in range(4):

            @pl.loop(1 if k == 3 else 0, 8)
            def _(j, half=half, k=k):
                @pl.when(jnp.logical_not(outer) | (k >= 2))
                def _():
                    deliver(half, k, lax.rem(me + j, 8)).wait_send()

        @pl.when(outer)
        def _(half=half):
            for k in range(2):
                for part in range(2):
                    hand(half, k, part).wait_send()

    @pl.loop(1, 8)
    def _(i):
        q = lax.rem(me + i, 8)
        share_near(q).wait_send()
        for part in range(2):
            share_far(part, q).wait_send()

    for part in range(2):
        for k in range(4):
            over_z(part, k).wait_send()
    for far in range(2):
        for part in range(2):
            for i in range(2):
                pass_on(far, part, i).wait_send()
    for ck in range(2):
        to_sibling(ck).wait_send()
    for k in range(4):
        for p in y_peers:
            alpha_copy(k, p).wait_send()
    for cp in sends:
        cp.wait_send()


VMEM = pl.BlockSpec(memory_space=pltpu.VMEM)
DMA = pltpu.SemaphoreType.DMA


def body(rows_alpha, rows_beta, filter_alpha, filter_beta):
    consts = [jnp.asarray(w) for w in dft_constants()]
    return pl.pallas_call(
        kernel,
        out_shape=jax.ShapeDtypeStruct((32, 8 * CHAN), F32),
        in_specs=[pl.BlockSpec(memory_space=pl.ANY)] * 2 + [VMEM] * 6,
        out_specs=VMEM,
        scratch_shapes=[
            pltpu.VMEM((2, 3, CHAN, TOK), BF),
            pltpu.VMEM((2, CHAN, 128), BF),
            pltpu.VMEM((2, CHAN, 128), BF),
            pltpu.VMEM((2, 2, 4, 4, 32, TAPS), F32),
            pltpu.VMEM((CHAN, TOK), F32),
            pltpu.VMEM((CHAN, TOK), BF),
            pltpu.VMEM((2, 8, 128, 128), BF),
            pltpu.VMEM((2, 8, 128, 128), BF),
            pltpu.VMEM((2, 2, 8, 128), F32),
            pltpu.VMEM((4, 2, 2, 8, 128), F32),
            pltpu.VMEM((8, 2, 3, 8, 128), F32),
            pltpu.VMEM((2, 2, 8, 128), F32),
            pltpu.VMEM((2, 4, 16, 128), F32),
            pltpu.VMEM((8 * TOK, 128), BF),
            pltpu.VMEM((CHAN, 128), BF),
            pltpu.VMEM((CHAN, 8 * TOK), BF),
            pltpu.VMEM((2, 8, 2, 128, 512), BF),
            pltpu.VMEM((2, CHAN, 512), BF),
            pltpu.VMEM((2, CHUNK, 512), F32),
            pltpu.VMEM((2, 2, CHUNK, 512), BF),
            pltpu.VMEM((2, 3, 8, 32, 512), BF),
            DMA((2,)), DMA((2,)), DMA((2, 3)), DMA((2, 4)), DMA((2, 3)), DMA((2, 4)), DMA((2,)), DMA((2,)),
            DMA((2, 3)), DMA((2, 4)), DMA((2, 8)), DMA((2, 8)),
            DMA((8,)), DMA((8,)), DMA((2, 8)), DMA((2, 8)), DMA((4, 3)), DMA((4, 4)), DMA((4, 4)), DMA((4, 4)),
            DMA((2, 4)), DMA((2, 4)), DMA((2, 2, 2, 2)), DMA((2, 3, 2, 2)), DMA((7,)), DMA((3, 4)),
            DMA((2, 2, 2)), DMA((2, 2, 2)), DMA((2, 4, 8)), DMA((2, 3, 8)), DMA((2,)), DMA((2, 2)),
        ],
        compiler_params=pltpu.CompilerParams(
            collective_id=0, has_side_effects=True, vmem_limit_bytes=56 * 2**20
        ),
        name="correlate",
    )(rows_alpha, rows_beta, filter_alpha, filter_beta, *consts)


def solution(mesh):
    placed = (
        P(None, "grp", "seq"),
        P(None, "grp", "seq"),
        P(("grp", "seq"), None),
        P(("grp", "seq"), None),
    )
    return jax.shard_map(
        body, mesh=mesh, in_specs=placed, out_specs=P(("grp", "seq"), None), check_vma=False
    )
```

```python
import jax
import jax.numpy as jnp
import ml_dtypes
import numpy as np
from jax import lax
from jax.experimental import pallas as pl
from jax.experimental.pallas import tpu as pltpu
from jax.sharding import PartitionSpec as P

MESH = pl.DeviceIdType.MESH
BF = jnp.bfloat16
F32 = jnp.float32
TOKENS = 8192
CHAN = 1024
TOK = 256
TAPS = 128
CHUNK = 256


def split_const(matrix):
    high = matrix.astype(ml_dtypes.bfloat16)
    low = (matrix - high.astype(np.float64)).astype(ml_dtypes.bfloat16)
    return high, low


def dft_constants():
    n = np.arange(256)[:, None]
    k = np.arange(128)[None, :] + 0.5
    angle = 2.0 * np.pi * n * k / 256.0
    forward = np.concatenate([np.cos(angle), -np.sin(angle)], axis=1)
    back = angle[128:].T
    inverse = np.concatenate([np.cos(back), -np.sin(back)], axis=0) / 128.0
    return split_const(forward) + split_const(inverse)


def split(value):
    high = value.astype(BF)
    low = (value - high.astype(F32)).astype(BF)
    return high, low


def dot3(value, w_high, w_low):
    high, low = split(value)
    total = jnp.dot(low, w_high, preferred_element_type=F32)
    total = total + jnp.dot(high, w_low, preferred_element_type=F32)
    return total + jnp.dot(high, w_high, preferred_element_type=F32)


def place():
    g = lax.axis_index("grp")
    s = lax.axis_index("seq")
    return g, s, g // 2, g % 2, s // 8, (s // 2) % 4, s % 2


def eye_mask():
    r = lax.broadcasted_iota(jnp.int32, (128, 128), 0)
    c = lax.broadcasted_iota(jnp.int32, (128, 128), 1)
    return r == c


def to_row(column, eye):
    return jnp.sum(jnp.where(eye, jnp.broadcast_to(column, (128, 128)), 0.0), axis=0, keepdims=True)


def to_column(row, eye):
    return jnp.sum(jnp.where(eye, jnp.broadcast_to(row, (128, 128)), 0.0), axis=1, keepdims=True)


def kernel(
    all_a, all_b, filt_a, filt_b, wf_hi, wf_lo, wi_hi, wi_lo, out,
    kept, edge, halo, taps, centred, z_a, z_b, across, own, level1, level2, shifts, panel, pick, sums, alpha, beta,
    partial, exact, passed, landed,
    h_send, h_recv, f1_send, f1_recv, f2_send, f2_recv, f3_send, f3_recv, s1_send, s1_recv, s2_send, s2_recv,
    y_send, y_recv, w_send, w_recv, a_send, a_recv, c_send, c_recv, z_send, z_recv, x_send, x_recv, p_send, p_recv, r_send, r_recv, o_send, o_recv,
    local, l_sem,
):
    g, s, x, zh, zl, y, c = place()
    me = y * 2 + c
    zl_peers = [lax.rem(zl + i, 4) for i in range(1, 4)]
    y_peers = [lax.rem(y + i, 4) for i in range(1, 4)]
    x_peers = [lax.rem(x + i, 4) for i in range(1, 4)]
    sibling = (g, zl * 8 + y * 2 + 1 - c)
    other = (x * 2 + 1 - zh, s)

    side = zl // 2
    mate = side * 4 + 1 - zl
    outer = (zl + 1) % 4 < 2

    def chunk_at(k):
        far, near = 3 - 3 * side + (k % 2) * (2 * side - 1), mate + (k % 2) * (zl - mate)
        return (1 - k // 2) * far + (k // 2) * near

    def seq(a, b, d):
        return (g, a * 8 + b * 2 + d)

    barrier = pltpu.get_barrier_semaphore()

    def greet(device):
        pl.semaphore_signal(barrier, inc=1, device_id=device, device_id_type=MESH)

    @pl.loop(1, 32)
    def _(i):
        greet((g, lax.rem(s + i, 32)))

    for p in x_peers:
        greet((p * 2 + zh, s))
    greet(other)
    rows_a, rows_b = kept.at[0], kept.at[1]
    loads = []
    for ck, whole in ((0, all_a), (1, all_b)):
        for part in ((1, 3), (0, 1)):
            at = pl.ds(part[0], part[1] - part[0])
            load = pltpu.make_async_copy(whole.at[at], kept.at[ck, at], l_sem.at[ck, part[0]])
            load.start()
            loads.append(load)
    taps[0, c, y, zl] = filt_a[...]
    taps[1, c, y, zl] = filt_b[...]
    for ck in range(2):
        loads[2 * ck].wait()
        edge[ck] = (kept[ck, 1, :, 128:].astype(F32) * kept[ck, 2, :, 128:].astype(F32)).astype(BF)
    pl.semaphore_wait(barrier, 35)

    def copy(src, dst, send, recv, device):
        return pltpu.make_async_remote_copy(
            src_ref=src, dst_ref=dst, send_sem=send, recv_sem=recv, device_id=device, device_id_type=MESH
        )

    sends = []

    def go(*args):
        cp = copy(*args)
        cp.start()
        sends.append(cp)

    def arrive(dst, recv):
        copy(dst, dst, h_send.at[0], recv, sibling).wait_recv()

    def columns(q):
        return pl.ds(pl.multiple_of(q * TOK, TOK), TOK)

    def channels(q):
        return pl.ds(pl.multiple_of(q * 128, 128), 128)

    def chunk(i):
        return pl.ds(pl.multiple_of(i * CHUNK, CHUNK), CHUNK)

    def halo_out(ck):
        go(edge.at[ck], halo.at[ck], h_send.at[ck], h_recv.at[ck], (g, lax.rem(s + 1, 32)))

    def taps_copy(ck, i, p):
        mine = taps.at[ck, c, y]
        return copy(mine, mine, f2_send.at[ck, i], f2_recv.at[ck, y], seq(zl, p, c))

    for ck in range(2):
        for i, p in enumerate(zl_peers):
            mine = taps.at[ck, c, y, zl]
            go(mine, mine, f1_send.at[ck, i], f1_recv.at[ck, zl], seq(p, y, c))
    halo_out(0)
    for ck in range(2):
        for p in zl_peers:
            arrive(taps.at[ck, c, y, p], f1_recv.at[ck, p])
        for i, p in enumerate(y_peers):
            cp = taps_copy(ck, i, p)
            cp.start()
            sends.append(cp)
        if ck == 0:
            halo_out(1)

    lane = lax.broadcasted_iota(jnp.int32, (8 * TOK, 128), 1)
    slot = lax.broadcasted_iota(jnp.int32, (8 * TOK, 128), 0) // TOK
    pick[...] = jnp.where((lane < 24) & (lane % 8 == slot), 1.0, 0.0).astype(BF)

    eye = eye_mask()
    has_halo = s > 0

    def convolve(ck, rows, i):
        at = chunk(i)
        product = rows[1, at, :].astype(F32) * rows[2, at, :].astype(F32)
        before = jnp.where(has_halo, halo[ck, at, :].astype(F32), 0.0)
        window = jnp.concatenate([before, product[:, :128]], axis=1)
        spectrum = dot3(jnp.concatenate([window, product], axis=0), wf_hi[...], wf_lo[...])
        f = jnp.concatenate([taps[ck, d, b, i] for b in range(4) for d in range(2)], axis=0)
        response = dot3(f, wf_hi[:128], wf_lo[:128])
        f_re, f_im = response[:, :128], response[:, 128:]
        parts = []
        for w in range(2):
            x_re = spectrum[w * CHUNK : (w + 1) * CHUNK, :128]
            x_im = spectrum[w * CHUNK : (w + 1) * CHUNK, 128:]
            parts.append(jnp.concatenate([x_re * f_re - x_im * f_im, x_re * f_im + x_im * f_re], axis=1))
        conv = dot3(jnp.concatenate(parts, axis=0), wi_hi[...], wi_lo[...])
        conv = jnp.concatenate([conv[:CHUNK], conv[CHUNK:]], axis=1)
        gated = rows[0, at, :].astype(F32) * conv
        average = jnp.sum(gated, axis=1, keepdims=True) * (1.0 / TOK)
        diff = gated - average
        squares = jnp.sum(diff * diff, axis=1, keepdims=True)
        for h in range(CHUNK // 128):
            own[ck, 0, pl.ds(i * 2 + h, 1), :] = to_row(average[h * 128 : (h + 1) * 128], eye)
            own[ck, 1, pl.ds(i * 2 + h, 1), :] = to_row(squares[h * 128 : (h + 1) * 128], eye)
        return diff

    def to_sibling(ck):
        return copy(taps.at[ck, c], taps.at[ck, c], f3_send.at[ck], f3_recv.at[ck], sibling)

    def filters_half(ck):
        for p in y_peers:
            arrive(taps.at[ck, c, p], f2_recv.at[ck, p])
        to_sibling(ck).start()

    def filters_rest(ck):
        arrive(taps.at[ck, 1 - c], f3_recv.at[ck])
        arrive(halo.at[ck], h_recv.at[ck])

    def over_z(part, k):
        at = pl.ds(lax.rem(y + 1 + k, 4) * 2, 2)
        return copy(z_b.at[part, at], across.at[part, at], z_send.at[part, k], z_recv.at[part, k], other)

    def share_near(q):
        dst = beta.at[zh, me, :, :, channels(x)]
        return copy(z_b.at[:, q], dst, y_send.at[q], y_recv.at[me], (g, zl * 8 + q))

    def share_far(part, q):
        dst = beta.at[1 - zh, me, part, :, channels(x)]
        return copy(across.at[part, q], dst, w_send.at[part, q], w_recv.at[part, me], (g, zl * 8 + q))

    def relay_z(part):
        for k in range(4):
            i = lax.rem(y + 1 + k, 4)
            arrive(across.at[part, pl.ds(i * 2, 2)], z_recv.at[part, k])
            for h in range(2):
                q = i * 2 + h

                @pl.when(q != me)
                def _(q=q):
                    share_far(part, q).start()

        keep = pltpu.make_async_copy(across.at[part, me], beta.at[1 - zh, me, part, :, channels(x)], local.at[0])
        keep.start()
        keep.wait()

    up, down = (lax.rem(x + 1, 4) * 2 + zh, s), (lax.rem(x + 3, 4) * 2 + zh, s)

    def piece(far, step, part, at=slice(None)):
        zz = 1 - zh if far else zh
        return beta.at[zz, at, part, :, channels(lax.rem(x + step, 4))]

    def spread_x(far, part):
        src = piece(far, 0, part)
        for i, device in enumerate((up, down)):
            go(src, src, x_send.at[far, i, part, 0], x_recv.at[far, 2 - 2 * i, part, 0], device)

    def pass_on(far, part, i):
        src = piece(far, 3 - 2 * i, part, pl.ds(4 * i, 4))
        return copy(src, src, x_send.at[far, i, part, 1], x_recv.at[far, 1, part, i], down if i else up)

    def relay_x(far, part):
        for i in range(2):
            arrive(piece(far, 3 - 2 * i, part), x_recv.at[far, 2 - 2 * i, part, 0])
            pass_on(far, part, i).start()

    def rest_x(far):
        for part in range(2):
            for i in range(2):
                arrive(piece(far, 2, part, pl.ds(4 * i, 4)), x_recv.at[far, 1, part, i])

    def level_z(ck):
        level1[zl, ck] = own[ck]
        for i, p in enumerate(zl_peers):
            go(own.at[ck], level1.at[zl, ck], s1_send.at[ck, i], s1_recv.at[ck, zl], seq(p, y, c))

    def merge(parts, count):
        mean = sum(m for m, _ in parts) * (1.0 / len(parts))
        square = sum(v for _, v in parts)
        return mean, square + count * sum((m - mean) * (m - mean) for m, _ in parts)

    def level_y(ck):
        for p in zl_peers:
            arrive(level1.at[p, ck], s1_recv.at[ck, p])
        mean, square = merge([(level1[p, ck, 0], level1[p, ck, 1]) for p in range(4)], TOK)
        level2[me, ck, 0] = mean
        level2[me, ck, 1] = square
        level2[me, ck, 2] = own[ck, 0]
        for i in range(1, 8):
            q = lax.rem(me + i, 8)
            mine = level2.at[me, ck]
            go(mine, mine, s2_send.at[ck, i], s2_recv.at[ck, me], (g, zl * 8 + q))

    def statistics(ck):
        for i in range(1, 8):
            q = lax.rem(me + i, 8)
            arrive(level2.at[q, ck], s2_recv.at[ck, q])
        mean, square = merge([(level2[q, ck, 0], level2[q, ck, 1]) for q in range(8)], 4 * TOK)
        shifts[ck, 0] = own[ck, 0] - mean if ck == 0 else mean
        shifts[ck, 1] = lax.rsqrt(square * (1.0 / TOKENS) + 1e-05)

    filters_half(0)
    filters_rest(0)
    loads[1].wait()

    @pl.loop(0, 4)
    def _(i):
        centred[chunk(i), :] = convolve(0, rows_a, i)

        @pl.when(i == 2)
        def _():
            filters_half(1)

    level_z(0)
    level_y(0)

    filters_rest(1)
    loads[3].wait()

    @pl.loop(0, 4)
    def _(k):
        i = lax.rem(y + 1 + k, 4)
        turned = convolve(1, rows_b, i).T.astype(BF)
        for h in range(2):
            for part in range(2):
                z_b[part, i * 2 + h] = turned[part * 128 : (part + 1) * 128, h * 128 : (h + 1) * 128]
        for h in range(2):
            q = i * 2 + h

            @pl.when(q != me)
            def _(q=q):
                share_near(q).start()

    keep_b = pltpu.make_async_copy(z_b.at[:, me], beta.at[zh, me, :, :, channels(x)], local.at[0])
    keep_b.start()
    level_z(1)
    statistics(0)

    def alpha_out(k):
        at = chunk(chunk_at(k))
        src, dst = z_a.at[at], alpha.at[at, columns(me)]
        for j, p in enumerate(y_peers):
            go(src, dst, a_send.at[k, j], a_recv.at[k, y], seq(zl, p, c))
        go(src, dst, c_send.at[k, y], c_recv.at[k, y], sibling)

    for k in range(4):
        for h in range(2):
            block = chunk_at(k) * 2 + h
            shift_c = to_column(shifts[0, 0, pl.ds(block, 1), :], eye)
            scale_c = to_column(shifts[0, 1, pl.ds(block, 1), :], eye)
            z_a[channels(block), :] = ((centred[channels(block), :] + shift_c) * scale_c).astype(BF)
    for k in range(4):
        over_z(0, k).start()
    level_y(1)
    alpha_out(0)
    alpha_out(1)
    keep_a = pltpu.make_async_copy(z_a, alpha.at[:, columns(me)], local.at[1])
    keep_a.start()

    keep_b.wait()
    for i in range(1, 8):
        q = lax.rem(me + i, 8)
        arrive(beta.at[zh, q, :, :, channels(x)], y_recv.at[q])
    for part in range(2):
        spread_x(0, part)
    relay_x(0, 0)
    for k in range(4):
        over_z(1, k).start()
    statistics(1)

    mean_b = shifts[1, 0, pl.ds(me, 1), :]
    for q in range(8):
        panel[zh, x, q : q + 1, :] = level2[q, 1, 2, pl.ds(me, 1), :] - mean_b
    panel[zh, x, 8:9, :] = shifts[1, 1, pl.ds(me, 1), :]
    panel[zh, x, 9:16, :] = jnp.zeros((7, 128), F32)
    mine = panel.at[zh, x]
    go(mine, mine, p_send.at[6], p_recv.at[1, x], other)
    for i, p in enumerate(x_peers):
        go(mine, mine, p_send.at[i], p_recv.at[0, x], (p * 2 + zh, s))

    def alpha_slot(k, p, d):
        return alpha.at[chunk(chunk_at(k)), columns(p * 2 + d)]

    def alpha_copy(k, p):
        got = alpha_slot(k, p, c)
        return copy(got, got, c_send.at[k, p], c_recv.at[k, p], sibling)

    def relay_alpha(k):
        for p in y_peers:
            arrive(alpha_slot(k, p, c), a_recv.at[k, p])
            alpha_copy(k, p).start()

    def far_in(part):
        for i in range(1, 8):
            q = lax.rem(me + i, 8)
            arrive(beta.at[1 - zh, q, part, :, channels(x)], w_recv.at[part, q])
        spread_x(1, part)

    relay_z(0)
    alpha_out(2)
    relay_x(0, 1)
    far_in(0)
    relay_alpha(0)
    relay_alpha(1)
    relay_z(1)
    alpha_out(3)
    relay_alpha(2)
    keep_a.wait()

    lane = lax.broadcasted_iota(jnp.int32, (CHUNK, 128), 1)
    low_lanes = (lane >= 8) & (lane < 16)

    def hand(half, k, part):
        rows = pl.ds(pl.multiple_of(chunk_at(k) * CHUNK + part * 128, 128), 128)
        return copy(
            partial.at[half, rows], passed.at[half, k, pl.ds(part * 128, 128)],
            r_send.at[half, k, part], r_recv.at[half, k, part], (g, mate * 8 + me),
        )

    def deliver(half, k, q):
        i = chunk_at(k)
        src = partial.at[half, pl.ds(pl.multiple_of((i * 8 + q) * 32, 32), 32)]
        kind = 2 * (1 - k // 2) + (k // 2) * (1 - k % 2)
        return copy(src, landed.at[half, kind, me], o_send.at[half, k, q], o_recv.at[half, kind, me], (g, i * 8 + q))

    def deliver_all(half, k):
        @pl.loop(0, 8)
        def _(j):
            deliver(half, k, lax.rem(me + j, 8)).start()

    def join(half, k):
        @pl.when(jnp.logical_not(outer))
        def _():
            for part in range(2):
                rows = pl.ds(part * 128, 128)
                arrive(passed.at[half, k, rows], r_recv.at[half, k, part])
                at = pl.ds(pl.multiple_of(chunk_at(k) * CHUNK + part * 128, 128), 128)
                partial[half, at, :] = (exact[k, rows, :] + passed[half, k, rows, :].astype(F32)).astype(BF)

                @pl.loop(0, 4)
                def _(j, part=part):
                    deliver(half, k, part * 4 + lax.rem(me + j, 4)).start()

    def columns_in(half):
        zz = zh if half == 0 else 1 - zh
        rest_x(half)
        for p in x_peers:
            arrive(panel.at[zz, p], p_recv.at[2 * half, p])
        delta = jnp.concatenate([panel[zz, p, 0:8, :] for p in range(4)], axis=1)
        weight = jnp.concatenate([panel[zz, p, 8:9, :] for p in range(4)], axis=1) * (1.0 / TOKENS)
        delta_hi = delta.astype(BF).astype(F32)
        spread = jnp.concatenate(
            [delta_hi, delta_hi, delta - delta_hi, jnp.zeros((104, 512), F32)], axis=0
        ).astype(BF)
        return zz, spread, weight

    def product(half, first, last, found):
        zz, spread, weight = found

        @pl.loop(first, last)
        def _(k):
            at = chunk(chunk_at(k))
            if half == 0:
                for p in range(4):
                    arrive(alpha_slot(k, p, 1 - c), c_recv.at[k, p])
                total = jnp.dot(alpha[at, :], pick[...], preferred_element_type=F32)
                total_hi = total.astype(BF).astype(F32)
                sums[at, :] = jnp.where(low_lanes, total - total_hi, total_hi).astype(BF)
            block = jnp.dot(alpha[at, :], beta[zz].reshape(8 * TOK, 512), preferred_element_type=F32)
            block = block + jnp.dot(sums[at, :], spread, preferred_element_type=F32)
            block = block * weight
            partial[half, at, :] = block.astype(BF)
            if first < 2:
                exact[k] = block

                @pl.when(outer)
                def _():
                    for part in range(2):
                        hand(half, k, part).start()

            else:

                @pl.when(k == 2)
                def _():
                    deliver_all(half, 2)

        if last == 4:

            @pl.loop(1, 8)
            def _(j):
                deliver(half, 3, lax.rem(me + j, 8)).start()

            landed[half, 0, me] = partial[half, pl.ds(pl.multiple_of(s * 32, 32), 32), :]

    found = columns_in(0)
    product(0, 0, 2, found)
    far_in(1)
    mine = panel.at[1 - zh, x]
    arrive(mine, p_recv.at[1, x])
    for i, p in enumerate(x_peers):
        go(mine, mine, p_send.at[3 + i], p_recv.at[2, x], (p * 2 + zh, s))
    relay_x(1, 0)
    product(0, 2, 3, found)
    join(0, 0)
    relay_alpha(3)
    relay_x(1, 1)
    join(0, 1)
    product(0, 3, 4, found)
    found = columns_in(1)
    product(1, 0, 2, found)
    product(1, 2, 4, found)
    join(1, 0)
    join(1, 1)

    for half in range(2):
        zz = zh if half == 0 else 1 - zh

        @pl.loop(1, 8)
        def _(j, half=half):
            q = lax.rem(me + j, 8)
            arrive(landed.at[half, 0, q], o_recv.at[half, 0, q])

        @pl.loop(0, 8)
        def _(q, half=half, zz=zz):
            for kind in (1, 2):
                arrive(landed.at[half, kind, q], o_recv.at[half, kind, q])
            total = landed[half, 0, q].astype(F32) + landed[half, 1, q].astype(F32)
            total = total + landed[half, 2, q].astype(F32)
            for p in range(4):
                at = pl.multiple_of((p * 2 + zz) * 1024 + q * 128, 128)
                out[:, pl.ds(at, 128)] = total[:, p * 128 : (p + 1) * 128]

    for half in range(2):
        for k in range(4):

            @pl.loop(1 if k == 3 else 0, 8)
            def _(j, half=half, k=k):
                @pl.when(jnp.logical_not(outer) | (k >= 2))
                def _():
                    deliver(half, k, lax.rem(me + j, 8)).wait_send()

        @pl.when(outer)
        def _(half=half):
            for k in range(2):
                for part in range(2):
                    hand(half, k, part).wait_send()

    @pl.loop(1, 8)
    def _(i):
        q = lax.rem(me + i, 8)
        share_near(q).wait_send()
        for part in range(2):
            share_far(part, q).wait_send()

    for part in range(2):
        for k in range(4):
            over_z(part, k).wait_send()
    for far in range(2):
        for part in range(2):
            for i in range(2):
                pass_on(far, part, i).wait_send()
    for ck in range(2):
        to_sibling(ck).wait_send()
    for k in range(4):
        for p in y_peers:
            alpha_copy(k, p).wait_send()
    for cp in sends:
        cp.wait_send()


VMEM = pl.BlockSpec(memory_space=pltpu.VMEM)
DMA = pltpu.SemaphoreType.DMA


def body(rows_alpha, rows_beta, filter_alpha, filter_beta):
    consts = [jnp.asarray(w) for w in dft_constants()]
    return pl.pallas_call(
        kernel,
        out_shape=jax.ShapeDtypeStruct((32, 8 * CHAN), F32),
        in_specs=[pl.BlockSpec(memory_space=pl.ANY)] * 2 + [VMEM] * 6,
        out_specs=VMEM,
        scratch_shapes=[
            pltpu.VMEM((2, 3, CHAN, TOK), BF),
            pltpu.VMEM((2, CHAN, 128), BF),
            pltpu.VMEM((2, CHAN, 128), BF),
            pltpu.VMEM((2, 2, 4, 4, 32, TAPS), F32),
            pltpu.VMEM((CHAN, TOK), F32),
            pltpu.VMEM((CHAN, TOK), BF),
            pltpu.VMEM((2, 8, 128, 128), BF),
            pltpu.VMEM((2, 8, 128, 128), BF),
            pltpu.VMEM((2, 2, 8, 128), F32),
            pltpu.VMEM((4, 2, 2, 8, 128), F32),
            pltpu.VMEM((8, 2, 3, 8, 128), F32),
            pltpu.VMEM((2, 2, 8, 128), F32),
            pltpu.VMEM((2, 4, 16, 128), F32),
            pltpu.VMEM((8 * TOK, 128), BF),
            pltpu.VMEM((CHAN, 128), BF),
            pltpu.VMEM((CHAN, 8 * TOK), BF),
            pltpu.VMEM((2, 8, 2, 128, 512), BF),
            pltpu.VMEM((2, CHAN, 512), BF),
            pltpu.VMEM((2, CHUNK, 512), F32),
            pltpu.VMEM((2, 2, CHUNK, 512), BF),
            pltpu.VMEM((2, 3, 8, 32, 512), BF),
            DMA((2,)), DMA((2,)), DMA((2, 3)), DMA((2, 4)), DMA((2, 3)), DMA((2, 4)), DMA((2,)), DMA((2,)),
            DMA((2, 3)), DMA((2, 4)), DMA((2, 8)), DMA((2, 8)),
            DMA((8,)), DMA((8,)), DMA((2, 8)), DMA((2, 8)), DMA((4, 3)), DMA((4, 4)), DMA((4, 4)), DMA((4, 4)),
            DMA((2, 4)), DMA((2, 4)), DMA((2, 2, 2, 2)), DMA((2, 3, 2, 2)), DMA((7,)), DMA((3, 4)),
            DMA((2, 2, 2)), DMA((2, 2, 2)), DMA((2, 4, 8)), DMA((2, 3, 8)), DMA((2,)), DMA((2, 2)),
        ],
        compiler_params=pltpu.CompilerParams(
            collective_id=0, has_side_effects=True, vmem_limit_bytes=56 * 2**20
        ),
        name="correlate",
    )(rows_alpha, rows_beta, filter_alpha, filter_beta, *consts)


def solution(mesh):
    placed = (
        P(None, "grp", "seq"),
        P(None, "grp", "seq"),
        P(("grp", "seq"), None),
        P(("grp", "seq"), None),
    )
    return jax.shard_map(
        body, mesh=mesh, in_specs=placed, out_specs=P(("grp", "seq"), None), check_vma=False
    )
```

```python
import jax
import jax.numpy as jnp
import ml_dtypes
import numpy as np
from jax import lax
from jax.experimental import pallas as pl
from jax.experimental.pallas import tpu as pltpu
from jax.sharding import PartitionSpec as P

MESH = pl.DeviceIdType.MESH
BF = jnp.bfloat16
F32 = jnp.float32
TOKENS = 8192
CHAN = 1024
TOK = 256
TAPS = 128
CHUNK = 256


def split_const(matrix):
    high = matrix.astype(ml_dtypes.bfloat16)
    low = (matrix - high.astype(np.float64)).astype(ml_dtypes.bfloat16)
    return high, low


def dft_constants():
    n = np.arange(256)[:, None]
    k = np.arange(128)[None, :] + 0.5
    angle = 2.0 * np.pi * n * k / 256.0
    forward = np.concatenate([np.cos(angle), -np.sin(angle)], axis=1)
    back = angle[128:].T
    inverse = np.concatenate([np.cos(back), -np.sin(back)], axis=0) / 128.0
    return split_const(forward) + split_const(inverse)


def split(value):
    high = value.astype(BF)
    low = (value - high.astype(F32)).astype(BF)
    return high, low


def dot3(value, w_high, w_low):
    high, low = split(value)
    total = jnp.dot(low, w_high, preferred_element_type=F32)
    total = total + jnp.dot(high, w_low, preferred_element_type=F32)
    return total + jnp.dot(high, w_high, preferred_element_type=F32)


def place():
    g = lax.axis_index("grp")
    s = lax.axis_index("seq")
    return g, s, g // 2, g % 2, s // 8, (s // 2) % 4, s % 2


def eye_mask():
    r = lax.broadcasted_iota(jnp.int32, (128, 128), 0)
    c = lax.broadcasted_iota(jnp.int32, (128, 128), 1)
    return r == c


def to_row(column, eye):
    return jnp.sum(jnp.where(eye, jnp.broadcast_to(column, (128, 128)), 0.0), axis=0, keepdims=True)


def to_column(row, eye):
    return jnp.sum(jnp.where(eye, jnp.broadcast_to(row, (128, 128)), 0.0), axis=1, keepdims=True)


def kernel(
    all_a, all_b, filt_a, filt_b, wf_hi, wf_lo, wi_hi, wi_lo, out,
    kept, edge, halo, taps, centred, z_a, z_b, across, own, level1, level2, shifts, panel, pick, sums, alpha, beta,
    partial, exact, passed, landed, result,
    h_send, h_recv, f1_send, f1_recv, f2_send, f2_recv, f3_send, f3_recv, s1_send, s1_recv, s2_send, s2_recv,
    y_send, y_recv, w_send, w_recv, a_send, a_recv, c_send, c_recv, z_send, z_recv, x_send, x_recv, p_send, p_recv, r_send, r_recv, o_send, o_recv,
    local, l_sem, done,
):
    g, s, x, zh, zl, y, c = place()
    me = y * 2 + c
    zl_peers = [lax.rem(zl + i, 4) for i in range(1, 4)]
    y_peers = [lax.rem(y + i, 4) for i in range(1, 4)]
    x_peers = [lax.rem(x + i, 4) for i in range(1, 4)]
    sibling = (g, zl * 8 + y * 2 + 1 - c)
    other = (x * 2 + 1 - zh, s)

    side = zl // 2
    mate = side * 4 + 1 - zl
    outer = (zl + 1) % 4 < 2

    def chunk_at(k):
        far, near = 3 - 3 * side + (k % 2) * (2 * side - 1), mate + (k % 2) * (zl - mate)
        return (1 - k // 2) * far + (k // 2) * near

    def seq(a, b, d):
        return (g, a * 8 + b * 2 + d)

    barrier = pltpu.get_barrier_semaphore()

    def greet(device):
        pl.semaphore_signal(barrier, inc=1, device_id=device, device_id_type=MESH)

    @pl.loop(1, 32)
    def _(i):
        greet((g, lax.rem(s + i, 32)))

    for p in x_peers:
        greet((p * 2 + zh, s))
    greet(other)
    rows_a, rows_b = kept.at[0], kept.at[1]
    loads = []
    for ck, whole in ((0, all_a), (1, all_b)):
        for part in ((1, 3), (0, 1)):
            at = pl.ds(part[0], part[1] - part[0])
            load = pltpu.make_async_copy(whole.at[at], kept.at[ck, at], l_sem.at[ck, part[0]])
            load.start()
            loads.append(load)
    taps[0, c, y, zl] = filt_a[...]
    taps[1, c, y, zl] = filt_b[...]
    for ck in range(2):
        loads[2 * ck].wait()
        edge[ck] = (kept[ck, 1, :, 128:].astype(F32) * kept[ck, 2, :, 128:].astype(F32)).astype(BF)
    pl.semaphore_wait(barrier, 35)

    def copy(src, dst, send, recv, device):
        return pltpu.make_async_remote_copy(
            src_ref=src, dst_ref=dst, send_sem=send, recv_sem=recv, device_id=device, device_id_type=MESH
        )

    sends = []

    def go(*args):
        cp = copy(*args)
        cp.start()
        sends.append(cp)

    def arrive(dst, recv):
        copy(dst, dst, h_send.at[0], recv, sibling).wait_recv()

    def columns(q):
        return pl.ds(pl.multiple_of(q * TOK, TOK), TOK)

    def channels(q):
        return pl.ds(pl.multiple_of(q * 128, 128), 128)

    def chunk(i):
        return pl.ds(pl.multiple_of(i * CHUNK, CHUNK), CHUNK)

    def halo_out(ck):
        go(edge.at[ck], halo.at[ck], h_send.at[ck], h_recv.at[ck], (g, lax.rem(s + 1, 32)))

    def taps_copy(ck, i, p):
        mine = taps.at[ck, c, y]
        return copy(mine, mine, f2_send.at[ck, i], f2_recv.at[ck, y], seq(zl, p, c))

    for ck in range(2):
        for i, p in enumerate(zl_peers):
            mine = taps.at[ck, c, y, zl]
            go(mine, mine, f1_send.at[ck, i], f1_recv.at[ck, zl], seq(p, y, c))
    halo_out(0)
    for ck in range(2):
        for p in zl_peers:
            arrive(taps.at[ck, c, y, p], f1_recv.at[ck, p])
        for i, p in enumerate(y_peers):
            cp = taps_copy(ck, i, p)
            cp.start()
            sends.append(cp)
        if ck == 0:
            halo_out(1)

    lane = lax.broadcasted_iota(jnp.int32, (8 * TOK, 128), 1)
    slot = lax.broadcasted_iota(jnp.int32, (8 * TOK, 128), 0) // TOK
    pick[...] = jnp.where((lane < 24) & (lane % 8 == slot), 1.0, 0.0).astype(BF)

    eye = eye_mask()
    has_halo = s > 0

    def convolve(ck, rows, i):
        at = chunk(i)
        product = rows[1, at, :].astype(F32) * rows[2, at, :].astype(F32)
        before = jnp.where(has_halo, halo[ck, at, :].astype(F32), 0.0)
        window = jnp.concatenate([before, product[:, :128]], axis=1)
        spectrum = dot3(jnp.concatenate([window, product], axis=0), wf_hi[...], wf_lo[...])
        f = jnp.concatenate([taps[ck, d, b, i] for b in range(4) for d in range(2)], axis=0)
        response = dot3(f, wf_hi[:128], wf_lo[:128])
        f_re, f_im = response[:, :128], response[:, 128:]
        parts = []
        for w in range(2):
            x_re = spectrum[w * CHUNK : (w + 1) * CHUNK, :128]
            x_im = spectrum[w * CHUNK : (w + 1) * CHUNK, 128:]
            parts.append(jnp.concatenate([x_re * f_re - x_im * f_im, x_re * f_im + x_im * f_re], axis=1))
        conv = dot3(jnp.concatenate(parts, axis=0), wi_hi[...], wi_lo[...])
        conv = jnp.concatenate([conv[:CHUNK], conv[CHUNK:]], axis=1)
        gated = rows[0, at, :].astype(F32) * conv
        average = jnp.sum(gated, axis=1, keepdims=True) * (1.0 / TOK)
        diff = gated - average
        squares = jnp.sum(diff * diff, axis=1, keepdims=True)
        for h in range(CHUNK // 128):
            own[ck, 0, pl.ds(i * 2 + h, 1), :] = to_row(average[h * 128 : (h + 1) * 128], eye)
            own[ck, 1, pl.ds(i * 2 + h, 1), :] = to_row(squares[h * 128 : (h + 1) * 128], eye)
        return diff

    def to_sibling(ck):
        return copy(taps.at[ck, c], taps.at[ck, c], f3_send.at[ck], f3_recv.at[ck], sibling)

    def filters_half(ck):
        for p in y_peers:
            arrive(taps.at[ck, c, p], f2_recv.at[ck, p])
        to_sibling(ck).start()

    def filters_rest(ck):
        arrive(taps.at[ck, 1 - c], f3_recv.at[ck])
        arrive(halo.at[ck], h_recv.at[ck])

    def over_z(part, k):
        at = pl.ds(lax.rem(y + 1 + k, 4) * 2, 2)
        return copy(z_b.at[part, at], across.at[part, at], z_send.at[part, k], z_recv.at[part, k], other)

    def share_near(q):
        dst = beta.at[zh, me, :, :, channels(x)]
        return copy(z_b.at[:, q], dst, y_send.at[q], y_recv.at[me], (g, zl * 8 + q))

    def share_far(part, q):
        dst = beta.at[1 - zh, me, part, :, channels(x)]
        return copy(across.at[part, q], dst, w_send.at[part, q], w_recv.at[part, me], (g, zl * 8 + q))

    def relay_z(part):
        for k in range(4):
            i = lax.rem(y + 1 + k, 4)
            arrive(across.at[part, pl.ds(i * 2, 2)], z_recv.at[part, k])
            for h in range(2):
                q = i * 2 + h

                @pl.when(q != me)
                def _(q=q):
                    share_far(part, q).start()

        keep = pltpu.make_async_copy(across.at[part, me], beta.at[1 - zh, me, part, :, channels(x)], local.at[0])
        keep.start()
        keep.wait()

    up, down = (lax.rem(x + 1, 4) * 2 + zh, s), (lax.rem(x + 3, 4) * 2 + zh, s)

    def piece(far, step, part, at=slice(None)):
        zz = 1 - zh if far else zh
        return beta.at[zz, at, part, :, channels(lax.rem(x + step, 4))]

    def spread_x(far, part):
        src = piece(far, 0, part)
        for i, device in enumerate((up, down)):
            go(src, src, x_send.at[far, i, part, 0], x_recv.at[far, 2 - 2 * i, part, 0], device)

    def pass_on(far, part, i):
        src = piece(far, 3 - 2 * i, part, pl.ds(4 * i, 4))
        return copy(src, src, x_send.at[far, i, part, 1], x_recv.at[far, 1, part, i], down if i else up)

    def relay_x(far, part):
        for i in range(2):
            arrive(piece(far, 3 - 2 * i, part), x_recv.at[far, 2 - 2 * i, part, 0])
            pass_on(far, part, i).start()

    def rest_x(far):
        for part in range(2):
            for i in range(2):
                arrive(piece(far, 2, part, pl.ds(4 * i, 4)), x_recv.at[far, 1, part, i])

    def level_z(ck):
        level1[zl, ck] = own[ck]
        for i, p in enumerate(zl_peers):
            go(own.at[ck], level1.at[zl, ck], s1_send.at[ck, i], s1_recv.at[ck, zl], seq(p, y, c))

    def merge(parts, count):
        mean = sum(m for m, _ in parts) * (1.0 / len(parts))
        square = sum(v for _, v in parts)
        return mean, square + count * sum((m - mean) * (m - mean) for m, _ in parts)

    def level_y(ck):
        for p in zl_peers:
            arrive(level1.at[p, ck], s1_recv.at[ck, p])
        mean, square = merge([(level1[p, ck, 0], level1[p, ck, 1]) for p in range(4)], TOK)
        level2[me, ck, 0] = mean
        level2[me, ck, 1] = square
        level2[me, ck, 2] = own[ck, 0]
        for i in range(1, 8):
            q = lax.rem(me + i, 8)
            mine = level2.at[me, ck]
            go(mine, mine, s2_send.at[ck, i], s2_recv.at[ck, me], (g, zl * 8 + q))

    def statistics(ck):
        for i in range(1, 8):
            q = lax.rem(me + i, 8)
            arrive(level2.at[q, ck], s2_recv.at[ck, q])
        mean, square = merge([(level2[q, ck, 0], level2[q, ck, 1]) for q in range(8)], 4 * TOK)
        shifts[ck, 0] = own[ck, 0] - mean if ck == 0 else mean
        shifts[ck, 1] = lax.rsqrt(square * (1.0 / TOKENS) + 1e-05)

    filters_half(0)
    filters_rest(0)
    loads[1].wait()

    @pl.loop(0, 4)
    def _(i):
        centred[chunk(i), :] = convolve(0, rows_a, i)

        @pl.when(i == 2)
        def _():
            filters_half(1)

    level_z(0)
    level_y(0)

    filters_rest(1)
    loads[3].wait()

    @pl.loop(0, 4)
    def _(k):
        i = lax.rem(y + 1 + k, 4)
        turned = convolve(1, rows_b, i).T.astype(BF)
        for h in range(2):
            for part in range(2):
                z_b[part, i * 2 + h] = turned[part * 128 : (part + 1) * 128, h * 128 : (h + 1) * 128]
        for h in range(2):
            q = i * 2 + h

            @pl.when(q != me)
            def _(q=q):
                share_near(q).start()

    keep_b = pltpu.make_async_copy(z_b.at[:, me], beta.at[zh, me, :, :, channels(x)], local.at[0])
    keep_b.start()
    level_z(1)
    statistics(0)

    def alpha_out(k):
        at = chunk(chunk_at(k))
        src, dst = z_a.at[at], alpha.at[at, columns(me)]
        for j, p in enumerate(y_peers):
            go(src, dst, a_send.at[k, j], a_recv.at[k, y], seq(zl, p, c))
        go(src, dst, c_send.at[k, y], c_recv.at[k, y], sibling)

    for k in range(4):
        for h in range(2):
            block = chunk_at(k) * 2 + h
            shift_c = to_column(shifts[0, 0, pl.ds(block, 1), :], eye)
            scale_c = to_column(shifts[0, 1, pl.ds(block, 1), :], eye)
            z_a[channels(block), :] = ((centred[channels(block), :] + shift_c) * scale_c).astype(BF)
    for k in range(4):
        over_z(0, k).start()
    level_y(1)
    alpha_out(0)
    alpha_out(1)
    keep_a = pltpu.make_async_copy(z_a, alpha.at[:, columns(me)], local.at[1])
    keep_a.start()

    keep_b.wait()
    for i in range(1, 8):
        q = lax.rem(me + i, 8)
        arrive(beta.at[zh, q, :, :, channels(x)], y_recv.at[q])
    for part in range(2):
        spread_x(0, part)
    relay_x(0, 0)
    for k in range(4):
        over_z(1, k).start()
    statistics(1)

    mean_b = shifts[1, 0, pl.ds(me, 1), :]
    for q in range(8):
        panel[zh, x, q : q + 1, :] = level2[q, 1, 2, pl.ds(me, 1), :] - mean_b
    panel[zh, x, 8:9, :] = shifts[1, 1, pl.ds(me, 1), :]
    panel[zh, x, 9:16, :] = jnp.zeros((7, 128), F32)
    mine = panel.at[zh, x]
    go(mine, mine, p_send.at[6], p_recv.at[1, x], other)
    for i, p in enumerate(x_peers):
        go(mine, mine, p_send.at[i], p_recv.at[0, x], (p * 2 + zh, s))

    def alpha_slot(k, p, d):
        return alpha.at[chunk(chunk_at(k)), columns(p * 2 + d)]

    def alpha_copy(k, p):
        got = alpha_slot(k, p, c)
        return copy(got, got, c_send.at[k, p], c_recv.at[k, p], sibling)

    def relay_alpha(k):
        for p in y_peers:
            arrive(alpha_slot(k, p, c), a_recv.at[k, p])
            alpha_copy(k, p).start()

    def far_in(part):
        for i in range(1, 8):
            q = lax.rem(me + i, 8)
            arrive(beta.at[1 - zh, q, part, :, channels(x)], w_recv.at[part, q])
        spread_x(1, part)

    relay_z(0)
    alpha_out(2)
    relay_x(0, 1)
    far_in(0)
    relay_alpha(0)
    relay_alpha(1)
    relay_z(1)
    alpha_out(3)
    relay_alpha(2)
    keep_a.wait()

    lane = lax.broadcasted_iota(jnp.int32, (CHUNK, 128), 1)
    low_lanes = (lane >= 8) & (lane < 16)

    def hand(half, k, part):
        rows = pl.ds(pl.multiple_of(chunk_at(k) * CHUNK + part * 128, 128), 128)
        return copy(
            partial.at[half, rows], passed.at[half, k, pl.ds(part * 128, 128)],
            r_send.at[half, k, part], r_recv.at[half, k, part], (g, mate * 8 + me),
        )

    def deliver(half, k, q):
        i = chunk_at(k)
        src = partial.at[half, pl.ds(pl.multiple_of((i * 8 + q) * 32, 32), 32)]
        kind = 2 * (1 - k // 2) + (k // 2) * (1 - k % 2)
        return copy(src, landed.at[half, kind, me], o_send.at[half, k, q], o_recv.at[half, kind, me], (g, i * 8 + q))

    def deliver_all(half, k):
        @pl.loop(0, 8)
        def _(j):
            deliver(half, k, lax.rem(me + j, 8)).start()

    def join(half, k):
        @pl.when(jnp.logical_not(outer))
        def _():
            for part in range(2):
                rows = pl.ds(part * 128, 128)
                arrive(passed.at[half, k, rows], r_recv.at[half, k, part])
                at = pl.ds(pl.multiple_of(chunk_at(k) * CHUNK + part * 128, 128), 128)
                partial[half, at, :] = (exact[k, rows, :] + passed[half, k, rows, :].astype(F32)).astype(BF)

                @pl.loop(0, 4)
                def _(j, part=part):
                    deliver(half, k, part * 4 + lax.rem(me + j, 4)).start()

    def columns_in(half):
        zz = zh if half == 0 else 1 - zh
        rest_x(half)
        for p in x_peers:
            arrive(panel.at[zz, p], p_recv.at[2 * half, p])
        delta = jnp.concatenate([panel[zz, p, 0:8, :] for p in range(4)], axis=1)
        weight = jnp.concatenate([panel[zz, p, 8:9, :] for p in range(4)], axis=1) * (1.0 / TOKENS)
        delta_hi = delta.astype(BF).astype(F32)
        spread = jnp.concatenate(
            [delta_hi, delta_hi, delta - delta_hi, jnp.zeros((104, 512), F32)], axis=0
        ).astype(BF)
        return zz, spread, weight

    def product(half, first, last, found):
        zz, spread, weight = found

        @pl.loop(first, last)
        def _(k):
            at = chunk(chunk_at(k))
            if half == 0:
                for p in range(4):
                    arrive(alpha_slot(k, p, 1 - c), c_recv.at[k, p])
                total = jnp.dot(alpha[at, :], pick[...], preferred_element_type=F32)
                total_hi = total.astype(BF).astype(F32)
                sums[at, :] = jnp.where(low_lanes, total - total_hi, total_hi).astype(BF)
            block = jnp.dot(alpha[at, :], beta[zz].reshape(8 * TOK, 512), preferred_element_type=F32)
            block = block + jnp.dot(sums[at, :], spread, preferred_element_type=F32)
            block = block * weight
            partial[half, at, :] = block.astype(BF)
            if first < 2:
                exact[k] = block

                @pl.when(outer)
                def _():
                    for part in range(2):
                        hand(half, k, part).start()

            else:

                @pl.when(k == 2)
                def _():
                    deliver_all(half, 2)

        if last == 4:

            @pl.loop(1, 8)
            def _(j):
                deliver(half, 3, lax.rem(me + j, 8)).start()

            landed[half, 0, me] = partial[half, pl.ds(pl.multiple_of(s * 32, 32), 32), :]

    found = columns_in(0)
    product(0, 0, 2, found)
    far_in(1)
    mine = panel.at[1 - zh, x]
    arrive(mine, p_recv.at[1, x])
    for i, p in enumerate(x_peers):
        go(mine, mine, p_send.at[3 + i], p_recv.at[2, x], (p * 2 + zh, s))
    relay_x(1, 0)
    product(0, 2, 3, found)
    join(0, 0)
    relay_alpha(3)
    relay_x(1, 1)
    join(0, 1)
    product(0, 3, 4, found)
    found = columns_in(1)
    product(1, 0, 2, found)
    product(1, 2, 4, found)
    join(1, 0)
    join(1, 1)

    writes = []
    for half in range(2):
        zz = zh if half == 0 else 1 - zh

        @pl.loop(1, 8)
        def _(j, half=half):
            q = lax.rem(me + j, 8)
            arrive(landed.at[half, 0, q], o_recv.at[half, 0, q])

        @pl.loop(0, 8)
        def _(q, half=half, zz=zz):
            for kind in (1, 2):
                arrive(landed.at[half, kind, q], o_recv.at[half, kind, q])
            total = landed[half, 0, q].astype(F32) + landed[half, 1, q].astype(F32)
            total = total + landed[half, 2, q].astype(F32)
            for p in range(4):
                at = pl.multiple_of((p * 2 + zz) * 1024 + q * 128, 128)
                result[:, pl.ds(at, 128)] = total[:, p * 128 : (p + 1) * 128]

        for p in range(4):
            at = pl.ds(pl.multiple_of((p * 2 + zz) * 1024, 1024), 1024)
            write = pltpu.make_async_copy(result.at[:, at], out.at[:, at], done.at[half, p])
            write.start()
            writes.append(write)

    for half in range(2):
        for k in range(4):

            @pl.loop(1 if k == 3 else 0, 8)
            def _(j, half=half, k=k):
                @pl.when(jnp.logical_not(outer) | (k >= 2))
                def _():
                    deliver(half, k, lax.rem(me + j, 8)).wait_send()

        @pl.when(outer)
        def _(half=half):
            for k in range(2):
                for part in range(2):
                    hand(half, k, part).wait_send()

    @pl.loop(1, 8)
    def _(i):
        q = lax.rem(me + i, 8)
        share_near(q).wait_send()
        for part in range(2):
            share_far(part, q).wait_send()

    for part in range(2):
        for k in range(4):
            over_z(part, k).wait_send()
    for far in range(2):
        for part in range(2):
            for i in range(2):
                pass_on(far, part, i).wait_send()
    for ck in range(2):
        to_sibling(ck).wait_send()
    for k in range(4):
        for p in y_peers:
            alpha_copy(k, p).wait_send()
    for cp in sends:
        cp.wait_send()
    for write in writes:
        write.wait()


VMEM = pl.BlockSpec(memory_space=pltpu.VMEM)
DMA = pltpu.SemaphoreType.DMA


def body(rows_alpha, rows_beta, filter_alpha, filter_beta):
    consts = [jnp.asarray(w) for w in dft_constants()]
    return pl.pallas_call(
        kernel,
        out_shape=jax.ShapeDtypeStruct((32, 8 * CHAN), F32),
        in_specs=[pl.BlockSpec(memory_space=pl.ANY)] * 2 + [VMEM] * 6,
        out_specs=pl.BlockSpec(memory_space=pl.ANY),
        scratch_shapes=[
            pltpu.VMEM((2, 3, CHAN, TOK), BF),
            pltpu.VMEM((2, CHAN, 128), BF),
            pltpu.VMEM((2, CHAN, 128), BF),
            pltpu.VMEM((2, 2, 4, 4, 32, TAPS), F32),
            pltpu.VMEM((CHAN, TOK), F32),
            pltpu.VMEM((CHAN, TOK), BF),
            pltpu.VMEM((2, 8, 128, 128), BF),
            pltpu.VMEM((2, 8, 128, 128), BF),
            pltpu.VMEM((2, 2, 8, 128), F32),
            pltpu.VMEM((4, 2, 2, 8, 128), F32),
            pltpu.VMEM((8, 2, 3, 8, 128), F32),
            pltpu.VMEM((2, 2, 8, 128), F32),
            pltpu.VMEM((2, 4, 16, 128), F32),
            pltpu.VMEM((8 * TOK, 128), BF),
            pltpu.VMEM((CHAN, 128), BF),
            pltpu.VMEM((CHAN, 8 * TOK), BF),
            pltpu.VMEM((2, 8, 2, 128, 512), BF),
            pltpu.VMEM((2, CHAN, 512), BF),
            pltpu.VMEM((2, CHUNK, 512), F32),
            pltpu.VMEM((2, 2, CHUNK, 512), BF),
            pltpu.VMEM((2, 3, 8, 32, 512), BF),
            pltpu.VMEM((32, 8 * CHAN), F32),
            DMA((2,)), DMA((2,)), DMA((2, 3)), DMA((2, 4)), DMA((2, 3)), DMA((2, 4)), DMA((2,)), DMA((2,)),
            DMA((2, 3)), DMA((2, 4)), DMA((2, 8)), DMA((2, 8)),
            DMA((8,)), DMA((8,)), DMA((2, 8)), DMA((2, 8)), DMA((4, 3)), DMA((4, 4)), DMA((4, 4)), DMA((4, 4)),
            DMA((2, 4)), DMA((2, 4)), DMA((2, 2, 2, 2)), DMA((2, 3, 2, 2)), DMA((7,)), DMA((3, 4)),
            DMA((2, 2, 2)), DMA((2, 2, 2)), DMA((2, 4, 8)), DMA((2, 3, 8)), DMA((2,)), DMA((2, 2)), DMA((2, 4)),
        ],
        compiler_params=pltpu.CompilerParams(
            collective_id=0, has_side_effects=True, vmem_limit_bytes=56 * 2**20
        ),
        name="correlate",
    )(rows_alpha, rows_beta, filter_alpha, filter_beta, *consts)


def solution(mesh):
    placed = (
        P(None, "grp", "seq"),
        P(None, "grp", "seq"),
        P(("grp", "seq"), None),
        P(("grp", "seq"), None),
    )
    return jax.shard_map(
        body, mesh=mesh, in_specs=placed, out_specs=P(("grp", "seq"), None), check_vma=False
    )
```
